128 devices in a mesh: rows: 64 (over y, x, z), chan: 2 (over core).
Axes of the slice: x: 4, y: 4, z: 4, core: 2. Of those that a mesh axis runs over, the one named last changes fastest.
Arguments:
- field: bfloat16 [32, 1024, 4096], P('chan', 'rows'), may hold values from -6 to 6
- spec_weight: float32 [2, 2, 32, 32, 128, 128], P(None, None, 'chan', None, 'rows'), may hold values from -0.75 to 0.75
- conv_weight: bfloat16 [2, 2, 3, 3, 16, 16], P(None, 'chan'), may hold values from -0.5 to 0.5
- bias: float32 [2, 32], P(None, 'chan'), may hold values from -4 to 4
Outputs:
- output_field: bfloat16 [32, 1024, 4096], P('chan', 'rows')
The draws below stay inside these ranges and needn't reach their ends.
All inputs are finite; a program needn't handle non-finite values.
Results may differ from the reference program's by a relative error of at most 0.024.
Values may be sent and summed in bfloat16 or wider, within the bound.
A program may use at most 128 MiB of HBM per device.

```python
import math
import jax
import jax.numpy as jnp
from jax import lax

C = 32
GROUPS = 2
CG = 16
M = 128
NY = 4096
LAYERS = 2
NX = 1024


def block_scale(key, dims, pieces, least, high):
    level = 1.0
    for position, shards_of in pieces:
        heights = jax.random.uniform(jax.random.fold_in(jax.random.fold_in(key, 6), position), (shards_of,), jnp.float32, least / len(pieces), high / len(pieces))
        level = level * jnp.repeat(jnp.exp(heights), dims[position] // shards_of).reshape((-1,) + (1,) * (len(dims) - 1 - position))
    return level


def scatter_about(key, shape, spread, most, cuts=(), kind=jnp.bfloat16):
    array = spread * jax.random.normal(key, shape, jnp.float32)
    if cuts:
        array = array * block_scale(key, shape, cuts, -0.22, 0.18)
    return jnp.clip(array, -most, most).astype(kind)


def setup_inputs(seed: int = 0) -> dict:
    key_list = jax.random.split(jax.random.key(seed), 5)
    field = scatter_about(key_list[0], (C, NX, NY), 1.0, 6.0, ((0, 2), (1, 64)))
    spec_weight = scatter_about(key_list[1], (LAYERS, 2, C, C, M, M), (2 * C) ** -0.5, 0.75, ((2, 2), (4, 64)), jnp.float32)
    conv_weight = scatter_about(key_list[2], (LAYERS, GROUPS, 3, 3, CG, CG), (9 * CG) ** -0.5, 0.5, ((1, 2),))
    bias = scatter_about(key_list[3], (LAYERS, C), 1.0, 4.0, ((1, 2),), jnp.float32)
    return {"field": field, "spec_weight": spec_weight, "conv_weight": conv_weight, "bias": bias}


TWO_PI = 2.0 * math.pi
HIGHEST_PRECISION = lax.Precision.HIGHEST

def phase_angles(count, first, freqs, length):
    positions = first + jnp.arange(count, dtype=jnp.int32)
    products = positions[:, None] * freqs[None, :] % length
    return products.astype(jnp.float32) * (TWO_PI / length)

def forward_table(columns, modes):
    angles = phase_angles(columns, 0, jnp.arange(modes, dtype=jnp.int32), columns)
    return jnp.stack([jnp.cos(angles), -jnp.sin(angles)], axis=2).reshape(columns, 2 * modes).astype(jnp.bfloat16)

def backward_table(columns, modes):
    orders = jnp.arange(modes, dtype=jnp.int32)
    angles = phase_angles(columns, 0, orders, columns)
    factor = jnp.where(orders == 0, 1.0, 2.0).astype(jnp.float32) / modes
    cosine = jnp.cos(angles).T * factor[:, None]
    sine = jnp.sin(angles).T * factor[:, None]
    return jnp.stack([cosine, -sine], axis=1).reshape(2 * modes, columns).astype(jnp.bfloat16)

def row_tables(count, first, all_rows, modes):
    indices = jnp.arange(modes, dtype=jnp.int32)
    freqs = jnp.where(indices < modes // 2, indices, all_rows - modes + indices).astype(jnp.int32)
    angles = phase_angles(count, first, freqs, all_rows)
    return (jnp.cos(angles).astype(jnp.bfloat16), jnp.sin(angles).astype(jnp.bfloat16))

def forward_rows(pairs, cosine, sine):
    cos_wide = cosine.astype(jnp.float32)
    sin_wide = sine.astype(jnp.float32)
    shaped = pairs.astype(jnp.float32).reshape(pairs.shape[0] // 2, 2, pairs.shape[1], pairs.shape[2])
    real_part = shaped[:, 0]
    imag_part = shaped[:, 1]
    mode_real = jnp.einsum('ycx,xk->yck', real_part, cos_wide, precision=HIGHEST_PRECISION) + jnp.einsum('ycx,xk->yck', imag_part, sin_wide, precision=HIGHEST_PRECISION)
    mode_imag = jnp.einsum('ycx,xk->yck', imag_part, cos_wide, precision=HIGHEST_PRECISION) - jnp.einsum('ycx,xk->yck', real_part, sin_wide, precision=HIGHEST_PRECISION)
    stacked = jnp.stack([mode_real, mode_imag], axis=1)
    return stacked.reshape(pairs.shape[0], pairs.shape[1], cosine.shape[1])

def mix_modes(modes_arr, weight):
    shaped = modes_arr.reshape(modes_arr.shape[0] // 2, 2, modes_arr.shape[1], modes_arr.shape[2])
    mode_real = jnp.transpose(shaped[:, 0], (1, 0, 2))[:, None]
    mode_imag = jnp.transpose(shaped[:, 1], (1, 0, 2))[:, None]
    mixed_real = lax.optimization_barrier(jnp.sum(weight[0] * mode_real - weight[1] * mode_imag, axis=0))
    mixed_imag = lax.optimization_barrier(jnp.sum(weight[0] * mode_imag + weight[1] * mode_real, axis=0))
    return (mixed_real, mixed_imag)

def back_rows(mixed_real, mixed_imag, cosine, sine):
    cos_wide = cosine.astype(jnp.float32)
    sin_wide = sine.astype(jnp.float32)
    real_wide = mixed_real.astype(jnp.float32)
    imag_wide = mixed_imag.astype(jnp.float32)
    back_real = jnp.einsum('oyk,xk->yox', real_wide, cos_wide, precision=HIGHEST_PRECISION) - jnp.einsum('oyk,xk->yox', imag_wide, sin_wide, precision=HIGHEST_PRECISION)
    back_imag = jnp.einsum('oyk,xk->yox', real_wide, sin_wide, precision=HIGHEST_PRECISION) + jnp.einsum('oyk,xk->yox', imag_wide, cos_wide, precision=HIGHEST_PRECISION)
    stacked = jnp.stack([back_real, back_imag], axis=1)
    return stacked.reshape(2 * mixed_real.shape[1], mixed_real.shape[0], cosine.shape[0]).astype(jnp.bfloat16)

def local_conv(group_field, taps):
    kernel = jnp.transpose(taps.astype(jnp.float32), (2, 3, 0, 1))
    result = lax.conv_general_dilated(group_field.astype(jnp.float32)[None], kernel, (1, 1), ((1, 1), (1, 1)), dimension_numbers=('NCHW', 'OIHW', 'NCHW'), precision=HIGHEST_PRECISION)
    return result[0]

def reference(field, spec_weight, conv_weight, bias):
    channels, all_rows, columns = field.shape
    group_width = channels // GROUPS
    fwd_table = forward_table(columns, M).astype(jnp.float32)
    bwd_table = backward_table(columns, M).astype(jnp.float32)
    cosine, sine = row_tables(all_rows, 0, all_rows, M)
    scale = 1.0 / math.sqrt(all_rows * columns)
    hidden_field = field
    for layer in range(LAYERS):
        row_sums = lax.dot_general(fwd_table, hidden_field.astype(jnp.float32), (((0,), (2,)), ((), ())), precision=HIGHEST_PRECISION)
        row_modes = (row_sums * scale).astype(jnp.bfloat16)
        modes_arr = forward_rows(row_modes, cosine, sine)
        mixed_real, mixed_imag = mix_modes(modes_arr, spec_weight[layer])
        back = back_rows(mixed_real.astype(jnp.bfloat16), mixed_imag.astype(jnp.bfloat16), cosine, sine)
        results = []
        for group in range(GROUPS):
            low = group * group_width
            high = low + group_width
            spectral = lax.dot_general(back[:, low:high].astype(jnp.float32), bwd_table, (((0,), (0,)), ((), ())), precision=HIGHEST_PRECISION)
            local = local_conv(hidden_field[low:high], conv_weight[layer, group])
            summed = spectral + local + bias[layer, low:high][:, None, None]
            results.append(jax.nn.gelu(summed, approximate=True).astype(jnp.bfloat16))
        hidden_field = jnp.concatenate(results, axis=0)
    return hidden_field
```

```python
import functools
import math

import jax
import jax.numpy as jnp
import ml_dtypes
import numpy as np
from jax import lax
from jax.experimental import pallas as pl
from jax.experimental.pallas import tpu as pltpu
from jax.sharding import PartitionSpec as P

M = 128
LAYERS = 2
N = 64
CG = 16
XR = 16
NY = 4096
NX = N * XR
CX = CG * XR
TILE = 512
CHUNKS = 4
F32 = jnp.float32
BF16 = jnp.bfloat16
MESH = pl.DeviceIdType.MESH


def np_angles(count, freqs, length):
    products = (np.arange(count, dtype=np.int64)[:, None] * freqs[None, :]) % length
    return products.astype(np.float32) * np.float32(2.0 * math.pi / length)


def column_table():
    angles = np_angles(NY, np.arange(M), NY)
    both = np.stack([np.cos(angles), -np.sin(angles)], axis=2).reshape(NY, 2 * M)
    return np.ascontiguousarray(both.T).astype(ml_dtypes.bfloat16)


def row_table():
    j = np.arange(M)
    freqs = np.where(j < M // 2, j, NX - M + j)
    angles = np_angles(NX, freqs, NX)
    cosine = np.cos(angles).astype(ml_dtypes.bfloat16).reshape(N, XR, M).transpose(1, 0, 2)
    sine = np.sin(angles).astype(ml_dtypes.bfloat16).reshape(N, XR, M).transpose(1, 0, 2)
    real = np.concatenate([cosine, -sine], axis=2)
    imag = np.concatenate([sine, cosine], axis=2)
    return np.stack([real, imag], axis=1).reshape(XR * 2 * N, 2 * M)


def dot(a, b):
    return lax.dot_general(a, b, (((1,), (0,)), ((), ())), preferred_element_type=F32)


def dot_nt(a, b):
    return lax.dot_general(a, b, (((1,), (1,)), ((), ())), preferred_element_type=F32)


def gelu(v):
    return 0.5 * v * (1.0 + jnp.tanh(0.7978845608 * (v + 0.044715 * (v * v * v))))


def iota(shape, dim):
    return lax.broadcasted_iota(jnp.int32, shape, dim)


def kernel(
    field,
    table,
    rtable,
    weight,
    taps,
    bias,
    out,
    h,
    ft,
    rt,
    wt,
    hm,
    hp,
    acc,
    modes,
    snd,
    rcv,
    blk,
    ysc,
    lhs,
    usc,
    vs,
    vr,
    vrow,
    spec,
    conv_main,
    conv_edge,
    e_snd,
    e_rcv,
    e3,
    ld_sem,
    a_send,
    a_recv,
    c_send,
    c_recv,
    e_send,
    e_recv,
    o_sem,
):
    me = lax.axis_index("rows")
    chan = lax.axis_index("chan")
    width = NY // CHUNKS

    loads = []
    for i in range(CHUNKS):
        cols = pl.ds(i * width, width)
        loads.append(
            (
                pltpu.make_async_copy(table.at[:, cols], ft.at[:, cols], ld_sem.at[2 * i]),
                pltpu.make_async_copy(field.at[:, cols], h.at[:, cols], ld_sem.at[2 * i + 1]),
            )
        )
    load_rt = pltpu.make_async_copy(rtable, rt, ld_sem.at[2 * CHUNKS])
    load_wt = pltpu.make_async_copy(weight, wt, ld_sem.at[2 * CHUNKS + 1])
    for one, two in loads:
        one.start()
        two.start()
    load_rt.start()
    load_wt.start()

    barrier = pltpu.get_barrier_semaphore()

    def greet(i, carry):
        pl.semaphore_signal(
            barrier, inc=1, device_id={"rows": lax.rem(me + i, N)}, device_id_type=MESH
        )
        return carry

    lax.fori_loop(1, N, greet, 0)
    pl.semaphore_signal(barrier, inc=1, device_id={"chan": 1 - chan}, device_id_type=MESH)

    def partner(i):
        y = lax.rem(me // 16 + i // 16, 4)
        x = lax.rem(me // 4 + i // 4, 4)
        z = lax.rem(me + i, 4)
        return y * 16 + x * 4 + z

    def exchange(index):
        src, dst = snd.at[index], rcv.at[index]

        def go(i, carry):
            d = partner(i)
            pltpu.make_async_remote_copy(
                src_ref=src.at[d],
                dst_ref=dst.at[me],
                send_sem=a_send.at[index],
                recv_sem=a_recv.at[index],
                device_id={"rows": d},
                device_id_type=MESH,
            ).start()
            return carry

        lax.fori_loop(1, N, go, 0)
        pltpu.make_async_copy(src.at[me], dst.at[me], a_recv.at[index]).start()

    def exchange_done(index):
        dst = rcv.at[index]
        pltpu.make_async_copy(dst, dst, a_recv.at[index]).wait()

    def edge_copies(layer):
        up = lax.rem(me + 1, N)
        down = lax.rem(me + N - 1, N)
        return [
            pltpu.make_async_remote_copy(
                src_ref=e_snd.at[layer, side],
                dst_ref=e_rcv.at[layer, side],
                send_sem=e_send.at[layer, side],
                recv_sem=e_recv.at[layer, side],
                device_id={"rows": to},
                device_id_type=MESH,
            )
            for side, to in ((0, up), (1, down))
        ]

    def pack_rows():
        shaped = modes[...].reshape(N // 2, 8, CX)
        a, b = shaped[:, :, :128], shaped[:, :, 128:]
        low = iota((N // 2, 8, 128), 1) < 4
        even = jnp.where(low, a, pltpu.roll(b, 4, 1))
        odd = jnp.where(low, pltpu.roll(a, 4, 1), b)
        return even.astype(BF16), odd.astype(BF16)

    def conv_matrices(layer):
        row = iota((CX, CX), 0) & (XR - 1)
        col = iota((CX, CX), 1) & (XR - 1)
        out_of = ((iota((CX, CG), 0) >> 4) == iota((CX, CG), 1)).astype(F32).astype(BF16)
        in_of = ((iota((CG, CX), 1) >> 4) == iota((CG, CX), 0)).astype(F32).astype(BF16)
        xr = iota((CX, CG), 0) & (XR - 1)
        edge = jnp.zeros((CX, 128), F32)
        for s in range(3):
            total = jnp.zeros((CX, CX), F32)
            for r in range(3):
                tap = dot(out_of, taps[layer, r, s])
                total = jnp.where(col == row + (r - 1), dot(tap.astype(BF16), in_of), total)
                if r != 1:
                    side = 0 if r == 0 else 1
                    at = 0 if r == 0 else XR - 1
                    outer = (me == 0) if r == 0 else (me == N - 1)
                    keep = jnp.where(outer, -1, at)
                    offset = s * 32 + side * CG
                    place = (iota((CG, 128), 1) == iota((CG, 128), 0) + offset).astype(F32)
                    part = jnp.where(xr == keep, tap, 0.0).astype(BF16)
                    edge = edge + dot(part, place.astype(BF16))
            conv_main[layer, s] = total.astype(BF16)
        conv_edge[layer] = edge.astype(BF16)

    def edges_out(layer):
        side = iota((32, CX), 0) >> 4
        want = (iota((32, CX), 0) & 15) * XR + jnp.where(side == 0, XR - 1, 0)
        pick = (iota((32, CX), 1) == want).astype(F32).astype(BF16)

        def step(t, carry):
            cols = pl.ds(pl.multiple_of(t * TILE, TILE), TILE)
            rows = dot(pick, h[:, cols]).astype(BF16)
            e_snd[layer, 0, :, cols] = rows[:CG]
            e_snd[layer, 1, :, cols] = rows[CG:]
            return carry

        lax.fori_loop(0, NY // TILE, step, 0)
        for copy in edge_copies(layer):
            copy.start()

    def shifted(block):
        wide = block.astype(F32)
        lane = iota(wide.shape, 1)
        before = jnp.where(lane == 0, 0.0, pltpu.roll(wide, 1, 1))
        after = jnp.where(lane == NY - 1, 0.0, pltpu.roll(wide, NY - 1, 1))
        return before.astype(BF16), after.astype(BF16)

    def shift_field():
        def step(i, carry):
            rows = pl.ds(pl.multiple_of(i * 16, 16), 16)
            before, after = shifted(h[rows, :])
            hm[rows, :] = before
            hp[rows, :] = after
            return carry

        lax.fori_loop(0, CX // 16, step, 0)

    def convolve(layer):
        for copy in edge_copies(layer):
            copy.wait()
        for side in range(2):
            block = e_rcv[layer, side]
            before, after = shifted(block)
            e3[pl.ds(side * CG, CG), :] = before
            e3[pl.ds(32 + side * CG, CG), :] = block
            e3[pl.ds(64 + side * CG, CG), :] = after
        e3[pl.ds(96, 32), :] = jnp.zeros((32, NY), BF16)

        def step(t, carry):
            cols = pl.ds(pl.multiple_of(t * TILE, TILE), TILE)
            total = dot(conv_main[layer, 0], hm[:, cols])
            total += dot(conv_main[layer, 1], h[:, cols])
            total += dot(conv_main[layer, 2], hp[:, cols])
            total += dot(conv_edge[layer], e3[:, cols])
            acc[:, cols] = total + bias[layer]
            return carry

        lax.fori_loop(0, NY // TILE, step, 0)

    def mix(layer):
        blk[...] = rcv[2 * layer].astype(F32).reshape(N * 8, 128)
        for kk in range(2):
            for half in range(2):
                parts = [blk[pl.ds(half * 4 + 2 * kk + p, N, stride=8), :] for p in range(2)]
                ysc[2 * kk + half] = jnp.concatenate(parts, axis=0).T
        for x in range(XR):
            rows = [ysc[i, pl.ds(x, 8, stride=XR), :] for i in range(4)]
            lhs[:, pl.ds(x * 128, 128)] = jnp.concatenate(rows, axis=0).astype(BF16)
        usc[...] = dot(lhs[...], rt[...])
        odd = (iota((8, 128), 0) & 1) == 1
        real = jnp.zeros((8, 8, 128), F32)
        imag = jnp.zeros((8, 8, 128), F32)
        for c in range(CG):
            ur, ui = [
                jnp.where(
                    odd,
                    jnp.broadcast_to(usc[pl.ds(CG + c, 1), pl.ds(p * 128, 128)], (8, 128)),
                    jnp.broadcast_to(usc[pl.ds(c, 1), pl.ds(p * 128, 128)], (8, 128)),
                )[None]
                for p in range(2)
            ]
            wr = wt[layer, 0, c].reshape(8, 8, 128)
            wi = wt[layer, 1, c].reshape(8, 8, 128)
            real += wr * ur - wi * ui
            imag += wr * ui + wi * ur
        vs[layer, :, 0] = real.reshape(2, 32, 128)
        vs[layer, :, 1] = imag.reshape(2, 32, 128)

    def mixed_copy(layer):
        return pltpu.make_async_remote_copy(
            src_ref=vs.at[layer, 1 - chan],
            dst_ref=vr.at[layer],
            send_sem=c_send.at[layer],
            recv_sem=c_recv.at[layer],
            device_id={"chan": 1 - chan},
            device_id_type=MESH,
        )

    def back_rows(layer):
        vrow[...] = vs[layer, chan] + vr[layer]
        mixed = jnp.concatenate(
            [
                jnp.concatenate([vrow[p, pl.ds(kk, CG, stride=2), :] for kk in range(2)], axis=0)
                for p in range(2)
            ],
            axis=1,
        ).astype(BF16)
        for x in range(XR):
            piece = dot_nt(mixed, rt[pl.ds(x * 128, 128), :])
            for i in range(4):
                ysc[i, pl.ds(x, 8, stride=XR), :] = piece[8 * i : 8 * i + 8]
        scale = 2.0 / (M * math.sqrt(NX * NY))
        for kk in range(2):
            first = jnp.where(me == 0, 0.5 * scale, scale) if kk == 0 else scale
            for half in range(2):
                flipped = ysc[2 * kk + half].T * first
                for p in range(2):
                    blk[pl.ds(half * 4 + 2 * kk + p, N, stride=8), :] = flipped[
                        p * N : p * N + N
                    ]
        snd[2 * layer + 1] = blk[...].reshape(N, 8, 128).astype(BF16)

    def spectral_rows(layer):
        wide = rcv[2 * layer + 1].astype(F32).reshape(N // 2, 2, 8, 128)
        even, odd = wide[:, 0], wide[:, 1]
        low = iota((N // 2, 8, 128), 1) < 4
        a = jnp.where(low, even, pltpu.roll(odd, 4, 1)).reshape(CX, 128)
        b = jnp.where(low, pltpu.roll(even, 4, 1), odd).reshape(CX, 128)
        spec[pl.ds(0, 128), :] = a.T.astype(BF16)
        spec[pl.ds(128, 128), :] = b.T.astype(BF16)

    def forward_send(layer):
        even, odd = pack_rows()
        view = snd.at[2 * layer]
        for i in range(N // 2):
            view[2 * i] = even[i]
            view[2 * i + 1] = odd[i]

    modes[...] = jnp.zeros_like(modes)
    for i in range(CHUNKS):
        cols = pl.ds(i * width, width)
        loads[i][0].wait()
        loads[i][1].wait()
        modes[...] += dot_nt(ft[:, cols], h[:, cols])

    for layer in range(LAYERS):
        forward_send(layer)
        if layer == 0:
            pl.semaphore_wait(barrier, N)
        exchange(2 * layer)
        edges_out(layer)
        if layer == 0:
            for each in range(LAYERS):
                conv_matrices(each)
            load_rt.wait()
            load_wt.wait()
        shift_field()
        exchange_done(2 * layer)
        mix(layer)
        mixed_copy(layer).start()
        mixed_copy(layer).wait()
        back_rows(layer)
        exchange(2 * layer + 1)
        convolve(layer)
        exchange_done(2 * layer + 1)
        spectral_rows(layer)
        last = layer == LAYERS - 1
        if not last:
            modes[...] = jnp.zeros_like(modes)

        def step(t, carry):
            cols = pl.ds(pl.multiple_of(t * TILE, TILE), TILE)
            value = gelu(acc[:, cols] + dot(spec[...], ft[:, cols])).astype(BF16)
            h[:, cols] = value
            if last:
                pltpu.make_async_copy(h.at[:, cols], out.at[:, cols], o_sem.at[t]).start()
            else:
                modes[...] += dot_nt(ft[:, cols], value)
            return carry

        lax.fori_loop(0, NY // TILE, step, 0)

    def drain(t, carry):
        cols = pl.ds(pl.multiple_of(t * TILE, TILE), TILE)
        pltpu.make_async_copy(h.at[:, cols], out.at[:, cols], o_sem.at[t]).wait()
        return carry

    lax.fori_loop(0, NY // TILE, drain, 0)
    for index in range(2 * LAYERS):
        sent = snd.at[index, pl.ds(0, N - 1)]
        pltpu.make_async_copy(sent, sent, a_send.at[index]).wait()


def body(field, spec_weight, conv_weight, bias):
    flat = field.reshape(CX, NY)
    weight = spec_weight.reshape(LAYERS, 2, CG, 64, 128)
    taps = conv_weight.reshape(LAYERS, 3, 3, CG, CG)
    wide_bias = jnp.broadcast_to(bias[:, :, None, None], (LAYERS, CG, XR, 1)).reshape(LAYERS, CX, 1)
    anywhere = pl.BlockSpec(memory_space=pl.ANY)
    vmem = pl.BlockSpec(memory_space=pltpu.VMEM)
    result = pl.pallas_call(
        kernel,
        out_shape=jax.ShapeDtypeStruct((CX, NY), BF16),
        in_specs=[anywhere, anywhere, anywhere, anywhere, vmem, vmem],
        out_specs=anywhere,
        scratch_shapes=[
            pltpu.VMEM((CX, NY), BF16),
            pltpu.VMEM((2 * M, NY), BF16),
            pltpu.VMEM((XR * 2 * N, 2 * M), BF16),
            pltpu.VMEM((LAYERS, 2, CG, 64, 128), F32),
            pltpu.VMEM((CX, NY), BF16),
            pltpu.VMEM((CX, NY), BF16),
            pltpu.VMEM((CX, NY), F32),
            pltpu.VMEM((2 * M, CX), F32),
            pltpu.VMEM((2 * LAYERS, N, 8, 128), BF16),
            pltpu.VMEM((2 * LAYERS, N, 8, 128), BF16),
            pltpu.VMEM((N * 8, 128), F32),
            pltpu.VMEM((4, 128, 128), F32),
            pltpu.VMEM((32, XR * 128), BF16),
            pltpu.VMEM((32, 256), F32),
            pltpu.VMEM((LAYERS, 2, 2, 32, 128), F32),
            pltpu.VMEM((LAYERS, 2, 32, 128), F32),
            pltpu.VMEM((2, 32, 128), F32),
            pltpu.VMEM((CX, 2 * M), BF16),
            pltpu.VMEM((LAYERS, 3, CX, CX), BF16),
            pltpu.VMEM((LAYERS, CX, 128), BF16),
            pltpu.VMEM((LAYERS, 2, CG, NY), BF16),
            pltpu.VMEM((LAYERS, 2, CG, NY), BF16),
            pltpu.VMEM((128, NY), BF16),
            pltpu.SemaphoreType.DMA((2 * CHUNKS + 2,)),
            pltpu.SemaphoreType.DMA((2 * LAYERS,)),
            pltpu.SemaphoreType.DMA((2 * LAYERS,)),
            pltpu.SemaphoreType.DMA((LAYERS,)),
            pltpu.SemaphoreType.DMA((LAYERS,)),
            pltpu.SemaphoreType.DMA((LAYERS, 2)),
            pltpu.SemaphoreType.DMA((LAYERS, 2)),
            pltpu.SemaphoreType.DMA((NY // TILE,)),
        ],
        compiler_params=pltpu.CompilerParams(
            collective_id=0, has_side_effects=True, vmem_limit_bytes=56 * 2**20
        ),
        cost_estimate=pl.CostEstimate(
            flops=6 * 10**9, bytes_accessed=10 * 2**20, transcendentals=2 * CX * NY
        ),
        name="fourier_layers",
    )(flat, jnp.asarray(column_table()), jnp.asarray(row_table()), weight, taps, wide_bias)
    return result.reshape(CG, XR, NY)


def solution(mesh):
    in_specs = (
        P("chan", "rows", None),
        P(None, None, "chan", None, "rows", None),
        P(None, "chan", None, None, None, None),
        P(None, "chan"),
    )
    out_specs = P("chan", "rows", None)
    return jax.shard_map(body, mesh=mesh, in_specs=in_specs, out_specs=out_specs, check_vma=False)
```

```python
import functools
import math

import jax
import jax.numpy as jnp
import ml_dtypes
import numpy as np
from jax import lax
from jax.experimental import pallas as pl
from jax.experimental.pallas import tpu as pltpu
from jax.sharding import PartitionSpec as P

M = 128
LAYERS = 2
N = 64
CG = 16
XR = 16
NY = 4096
NX = N * XR
CX = CG * XR
TILE = 1024
TILES = NY // TILE
CHUNKS = 4
F32 = jnp.float32
BF16 = jnp.bfloat16
MESH = pl.DeviceIdType.MESH


def hops(offset):
    return sum(min(d, 4 - d) for d in offset)


OFFSETS = sorted(
    [(y, x, z) for y in range(4) for x in range(4) for z in range(4)][1:],
    key=lambda offset: -hops(offset),
)


def np_angles(count, freqs, length):
    products = (np.arange(count, dtype=np.int64)[:, None] * freqs[None, :]) % length
    return products.astype(np.float32) * np.float32(2.0 * math.pi / length)


def column_table():
    angles = np_angles(NY, np.arange(M), NY)
    both = np.stack([np.cos(angles), -np.sin(angles)], axis=2).reshape(NY, 2 * M)
    return np.ascontiguousarray(both.T).astype(ml_dtypes.bfloat16)


def row_table():
    j = np.arange(M)
    freqs = np.where(j < M // 2, j, NX - M + j)
    angles = np_angles(NX, freqs, NX)
    cosine = np.cos(angles).astype(ml_dtypes.bfloat16).reshape(N, XR, M).transpose(1, 0, 2)
    sine = np.sin(angles).astype(ml_dtypes.bfloat16).reshape(N, XR, M).transpose(1, 0, 2)
    real = np.concatenate([cosine, -sine], axis=2)
    imag = np.concatenate([sine, cosine], axis=2)
    return np.stack([real, imag], axis=1).reshape(XR * 2 * N, 2 * M)


def dot(a, b):
    return lax.dot_general(a, b, (((1,), (0,)), ((), ())), preferred_element_type=F32)


def dot_nt(a, b):
    return lax.dot_general(a, b, (((1,), (1,)), ((), ())), preferred_element_type=F32)


def gelu(v):
    return 0.5 * v * (1.0 + jnp.tanh(0.7978845608 * (v + 0.044715 * (v * v * v))))


def iota(shape, dim):
    return lax.broadcasted_iota(jnp.int32, shape, dim)


def kernel(
    field,
    table,
    rtable,
    weight,
    taps_any,
    bias_any,
    out,
    h,
    ft,
    rt,
    wt,
    taps,
    bias,
    bias_col,
    hm,
    hp,
    acc,
    modes,
    snd,
    rcv,
    blk,
    ysc,
    lhs,
    usc,
    vs,
    vr,
    vrow,
    spec,
    conv_main,
    conv_edge,
    e_snd,
    e_rcv,
    e3,
    ld_sem,
    a_send,
    a_recv,
    c_send,
    c_recv,
    e_send,
    e_recv,
    o_sem,
):
    me = lax.axis_index("rows")
    chan = lax.axis_index("chan")
    width = NY // CHUNKS

    loads = []
    for i in range(CHUNKS):
        cols = pl.ds(i * width, width)
        loads.append(
            (
                pltpu.make_async_copy(table.at[:, cols], ft.at[:, cols], ld_sem.at[2 * i]),
                pltpu.make_async_copy(field.at[:, cols], h.at[:, cols], ld_sem.at[2 * i + 1]),
            )
        )
    load_rt = pltpu.make_async_copy(rtable, rt, ld_sem.at[2 * CHUNKS])
    load_wt = pltpu.make_async_copy(weight, wt, ld_sem.at[2 * CHUNKS + 1])
    load_taps = pltpu.make_async_copy(taps_any, taps, ld_sem.at[2 * CHUNKS + 2])
    load_bias = pltpu.make_async_copy(bias_any, bias, ld_sem.at[2 * CHUNKS + 3])
    for one, two in loads:
        one.start()
        two.start()
    load_taps.start()
    load_bias.start()
    load_rt.start()
    load_wt.start()

    barrier = pltpu.get_barrier_semaphore()

    def greet(i, carry):
        pl.semaphore_signal(
            barrier, inc=1, device_id={"rows": lax.rem(me + i, N)}, device_id_type=MESH
        )
        return carry

    lax.fori_loop(1, N, greet, 0)
    pl.semaphore_signal(barrier, inc=1, device_id={"chan": 1 - chan}, device_id_type=MESH)

    ys = [lax.rem(me // 16 + i, 4) * 16 for i in range(4)]
    xs = [lax.rem(me // 4 + i, 4) * 4 for i in range(4)]
    zs = [lax.rem(me + i, 4) for i in range(4)]

    def exchange(index):
        src, dst = snd.at[index], rcv.at[index]
        for y, x, z in OFFSETS:
            d = ys[y] + xs[x] + zs[z]
            pltpu.make_async_remote_copy(
                src_ref=src.at[d],
                dst_ref=dst.at[me],
                send_sem=a_send.at[index],
                recv_sem=a_recv.at[index],
                device_id={"rows": d},
                device_id_type=MESH,
            ).start()
        pltpu.make_async_copy(src.at[me], dst.at[me], a_recv.at[index]).start()

    def exchange_done(index):
        dst = rcv.at[index]
        pltpu.make_async_copy(dst, dst, a_recv.at[index]).wait()

    def edge_copies(layer):
        up = lax.rem(me + 1, N)
        down = lax.rem(me + N - 1, N)
        return [
            pltpu.make_async_remote_copy(
                src_ref=e_snd.at[layer, side],
                dst_ref=e_rcv.at[layer, side],
                send_sem=e_send.at[layer, side],
                recv_sem=e_recv.at[layer, side],
                device_id={"rows": to},
                device_id_type=MESH,
            )
            for side, to in ((0, up), (1, down))
        ]

    def pack_rows():
        shaped = modes[...].reshape(N // 2, 8, CX)
        a, b = shaped[:, :, :128], shaped[:, :, 128:]
        low = iota((N // 2, 8, 128), 1) < 4
        even = jnp.where(low, a, pltpu.roll(b, 4, 1))
        odd = jnp.where(low, pltpu.roll(a, 4, 1), b)
        return even.astype(BF16), odd.astype(BF16)

    def conv_matrices(layer):
        row = iota((CX, CX), 0) & (XR - 1)
        col = iota((CX, CX), 1) & (XR - 1)
        out_of = ((iota((CX, CG), 0) >> 4) == iota((CX, CG), 1)).astype(F32).astype(BF16)
        in_of = ((iota((CG, CX), 1) >> 4) == iota((CG, CX), 0)).astype(F32).astype(BF16)
        xr = iota((CX, CG), 0) & (XR - 1)
        edge = jnp.zeros((CX, 128), F32)
        for s in range(3):
            total = jnp.zeros((CX, CX), F32)
            for r in range(3):
                tap = dot(out_of, taps[layer, r, s])
                total = jnp.where(col == row + (r - 1), dot(tap.astype(BF16), in_of), total)
                if r != 1:
                    side = 0 if r == 0 else 1
                    at = 0 if r == 0 else XR - 1
                    outer = (me == 0) if r == 0 else (me == N - 1)
                    keep = jnp.where(outer, -1, at)
                    offset = s * 32 + side * CG
                    place = (iota((CG, 128), 1) == iota((CG, 128), 0) + offset).astype(F32)
                    part = jnp.where(xr == keep, tap, 0.0).astype(BF16)
                    edge = edge + dot(part, place.astype(BF16))
            conv_main[layer, s] = total.astype(BF16)
        conv_edge[layer] = edge.astype(BF16)
        of = iota((CX, CG), 0) >> 4
        chosen = jnp.where(of == iota((CX, CG), 1), bias[pl.ds(layer, 1), :], 0.0)
        bias_col[layer] = jnp.sum(chosen, axis=1, keepdims=True)

    def edges_out(layer):
        side = iota((32, CX), 0) >> 4
        want = (iota((32, CX), 0) & 15) * XR + jnp.where(side == 0, XR - 1, 0)
        pick = (iota((32, CX), 1) == want).astype(F32).astype(BF16)

        def step(t, carry):
            cols = pl.ds(pl.multiple_of(t * TILE, TILE), TILE)
            rows = dot(pick, h[:, cols]).astype(BF16)
            e_snd[layer, 0, :, cols] = rows[:CG]
            e_snd[layer, 1, :, cols] = rows[CG:]
            return carry

        lax.fori_loop(0, TILES, step, 0, unroll=True)
        for copy in edge_copies(layer):
            copy.start()

    def shifted(block):
        zero = jnp.zeros((block.shape[0], 1), BF16)
        before = jnp.concatenate([zero, block[:, : NY - 1]], axis=1)
        after = jnp.concatenate([block[:, 1:], zero], axis=1)
        return before, after

    def shift_field():
        def step(i, carry):
            rows = pl.ds(pl.multiple_of(i * 16, 16), 16)
            before, after = shifted(h[rows, :])
            hm[rows, :] = before
            hp[rows, :] = after
            return carry

        lax.fori_loop(0, CX // 16, step, 0)

    def convolve(layer):
        for copy in edge_copies(layer):
            copy.wait()
        for side in range(2):
            block = e_rcv[layer, side]
            before, after = shifted(block)
            e3[pl.ds(side * CG, CG), :] = before
            e3[pl.ds(32 + side * CG, CG), :] = block
            e3[pl.ds(64 + side * CG, CG), :] = after
        e3[pl.ds(96, 32), :] = jnp.zeros((32, NY), BF16)

        def step(t, carry):
            cols = pl.ds(pl.multiple_of(t * TILE, TILE), TILE)
            total = dot(conv_main[layer, 0], hm[:, cols])
            total += dot(conv_main[layer, 1], h[:, cols])
            total += dot(conv_main[layer, 2], hp[:, cols])
            total += dot(conv_edge[layer], e3[:, cols])
            acc[:, cols] = total + bias_col[layer]
            return carry

        lax.fori_loop(0, TILES, step, 0, unroll=True)

    def mix(layer):
        blk[...] = rcv[2 * layer].astype(F32).reshape(N * 8, 128)
        for kk in range(2):
            for half in range(2):
                parts = [blk[pl.ds(half * 4 + 2 * kk + p, N, stride=8), :] for p in range(2)]
                ysc[2 * kk + half] = jnp.concatenate(parts, axis=0).T
        for x in range(XR):
            rows = [ysc[i, pl.ds(x, 8, stride=XR), :] for i in range(4)]
            lhs[:, pl.ds(x * 128, 128)] = jnp.concatenate(rows, axis=0).astype(BF16)
        usc[...] = dot(lhs[...], rt[...])
        odd = (iota((8, 128), 0) & 1) == 1
        real = jnp.zeros((8, 8, 128), F32)
        imag = jnp.zeros((8, 8, 128), F32)
        for c in range(CG):
            ur, ui = [
                jnp.where(
                    odd,
                    jnp.broadcast_to(usc[pl.ds(CG + c, 1), pl.ds(p * 128, 128)], (8, 128)),
                    jnp.broadcast_to(usc[pl.ds(c, 1), pl.ds(p * 128, 128)], (8, 128)),
                )[None]
                for p in range(2)
            ]
            wr = wt[layer, 0, c].reshape(8, 8, 128)
            wi = wt[layer, 1, c].reshape(8, 8, 128)
            real += wr * ur - wi * ui
            imag += wr * ui + wi * ur
        vs[layer, :, 0] = real.reshape(2, 32, 128)
        vs[layer, :, 1] = imag.reshape(2, 32, 128)

    def mixed_copy(layer):
        return pltpu.make_async_remote_copy(
            src_ref=vs.at[layer, 1 - chan],
            dst_ref=vr.at[layer],
            send_sem=c_send.at[layer],
            recv_sem=c_recv.at[layer],
            device_id={"chan": 1 - chan},
            device_id_type=MESH,
        )

    def back_rows(layer):
        vrow[...] = vs[layer, chan] + vr[layer]
        mixed = jnp.concatenate(
            [
                jnp.concatenate([vrow[p, pl.ds(kk, CG, stride=2), :] for kk in range(2)], axis=0)
                for p in range(2)
            ],
            axis=1,
        ).astype(BF16)
        for x in range(XR):
            piece = dot_nt(mixed, rt[pl.ds(x * 128, 128), :])
            for i in range(4):
                ysc[i, pl.ds(x, 8, stride=XR), :] = piece[8 * i : 8 * i + 8]
        scale = 2.0 / (M * math.sqrt(NX * NY))
        for kk in range(2):
            first = jnp.where(me == 0, 0.5 * scale, scale) if kk == 0 else scale
            for half in range(2):
                flipped = ysc[2 * kk + half].T * first
                for p in range(2):
                    blk[pl.ds(half * 4 + 2 * kk + p, N, stride=8), :] = flipped[
                        p * N : p * N + N
                    ]
        snd[2 * layer + 1] = blk[...].reshape(N, 8, 128).astype(BF16)

    def spectral_rows(layer):
        wide = rcv[2 * layer + 1].astype(F32).reshape(N // 2, 2, 8, 128)
        even, odd = wide[:, 0], wide[:, 1]
        low = iota((N // 2, 8, 128), 1) < 4
        a = jnp.where(low, even, pltpu.roll(odd, 4, 1)).reshape(CX, 128)
        b = jnp.where(low, pltpu.roll(even, 4, 1), odd).reshape(CX, 128)
        spec[pl.ds(0, 128), :] = a.T.astype(BF16)
        spec[pl.ds(128, 128), :] = b.T.astype(BF16)

    def forward_send(layer):
        even, odd = pack_rows()
        view = snd.at[2 * layer]
        for i in range(N // 2):
            view[2 * i] = even[i]
            view[2 * i + 1] = odd[i]

    modes[...] = jnp.zeros_like(modes)
    for i in range(CHUNKS):
        cols = pl.ds(i * width, width)
        loads[i][0].wait()
        loads[i][1].wait()
        modes[...] += dot_nt(ft[:, cols], h[:, cols])

    for layer in range(LAYERS):
        forward_send(layer)
        if layer == 0:
            pl.semaphore_wait(barrier, N)
        exchange(2 * layer)
        edges_out(layer)
        if layer == 0:
            load_taps.wait()
            load_bias.wait()
            load_rt.wait()
            load_wt.wait()
        shift_field()
        conv_matrices(layer)
        exchange_done(2 * layer)
        mix(layer)
        mixed_copy(layer).start()
        mixed_copy(layer).wait()
        back_rows(layer)
        exchange(2 * layer + 1)
        convolve(layer)
        exchange_done(2 * layer + 1)
        spectral_rows(layer)
        last = layer == LAYERS - 1
        if not last:
            modes[...] = jnp.zeros_like(modes)

        def step(t, carry):
            cols = pl.ds(pl.multiple_of(t * TILE, TILE), TILE)
            value = gelu(acc[:, cols] + dot(spec[...], ft[:, cols])).astype(BF16)
            h[:, cols] = value
            if last:
                pltpu.make_async_copy(h.at[:, cols], out.at[:, cols], o_sem.at[t]).start()
            else:
                modes[...] += dot_nt(ft[:, cols], value)
            return carry

        lax.fori_loop(0, TILES, step, 0, unroll=True)

    def drain(t, carry):
        cols = pl.ds(pl.multiple_of(t * TILE, TILE), TILE)
        pltpu.make_async_copy(h.at[:, cols], out.at[:, cols], o_sem.at[t]).wait()
        return carry

    lax.fori_loop(0, TILES, drain, 0)
    for index in range(2 * LAYERS):
        sent = snd.at[index, pl.ds(0, N - 1)]
        pltpu.make_async_copy(sent, sent, a_send.at[index]).wait()


def body(field, spec_weight, conv_weight, bias):
    flat = field.reshape(CX, NY)
    weight = spec_weight.reshape(LAYERS, 2, CG, 64, 128)
    taps = conv_weight.reshape(LAYERS, 3, 3, CG, CG)
    anywhere = pl.BlockSpec(memory_space=pl.ANY)
    result = pl.pallas_call(
        kernel,
        out_shape=jax.ShapeDtypeStruct((CX, NY), BF16),
        in_specs=[anywhere] * 6,
        out_specs=anywhere,
        scratch_shapes=[
            pltpu.VMEM((CX, NY), BF16),
            pltpu.VMEM((2 * M, NY), BF16),
            pltpu.VMEM((XR * 2 * N, 2 * M), BF16),
            pltpu.VMEM((LAYERS, 2, CG, 64, 128), F32),
            pltpu.VMEM((LAYERS, 3, 3, CG, CG), BF16),
            pltpu.VMEM((LAYERS, CG), F32),
            pltpu.VMEM((LAYERS, CX, 1), F32),
            pltpu.VMEM((CX, NY), BF16),
            pltpu.VMEM((CX, NY), BF16),
            pltpu.VMEM((CX, NY), F32),
            pltpu.VMEM((2 * M, CX), F32),
            pltpu.VMEM((2 * LAYERS, N, 8, 128), BF16),
            pltpu.VMEM((2 * LAYERS, N, 8, 128), BF16),
            pltpu.VMEM((N * 8, 128), F32),
            pltpu.VMEM((4, 128, 128), F32),
            pltpu.VMEM((32, XR * 128), BF16),
            pltpu.VMEM((32, 256), F32),
            pltpu.VMEM((LAYERS, 2, 2, 32, 128), F32),
            pltpu.VMEM((LAYERS, 2, 32, 128), F32),
            pltpu.VMEM((2, 32, 128), F32),
            pltpu.VMEM((CX, 2 * M), BF16),
            pltpu.VMEM((LAYERS, 3, CX, CX), BF16),
            pltpu.VMEM((LAYERS, CX, 128), BF16),
            pltpu.VMEM((LAYERS, 2, CG, NY), BF16),
            pltpu.VMEM((LAYERS, 2, CG, NY), BF16),
            pltpu.VMEM((128, NY), BF16),
            pltpu.SemaphoreType.DMA((2 * CHUNKS + 4,)),
            pltpu.SemaphoreType.DMA((2 * LAYERS,)),
            pltpu.SemaphoreType.DMA((2 * LAYERS,)),
            pltpu.SemaphoreType.DMA((LAYERS,)),
            pltpu.SemaphoreType.DMA((LAYERS,)),
            pltpu.SemaphoreType.DMA((LAYERS, 2)),
            pltpu.SemaphoreType.DMA((LAYERS, 2)),
            pltpu.SemaphoreType.DMA((TILES,)),
        ],
        compiler_params=pltpu.CompilerParams(
            collective_id=0, has_side_effects=True, vmem_limit_bytes=56 * 2**20
        ),
        cost_estimate=pl.CostEstimate(
            flops=6 * 10**9, bytes_accessed=10 * 2**20, transcendentals=2 * CX * NY
        ),
        name="fourier_layers",
    )(flat, jnp.asarray(column_table()), jnp.asarray(row_table()), weight, taps, bias)
    return result.reshape(CG, XR, NY)


def solution(mesh):
    in_specs = (
        P("chan", "rows", None),
        P(None, None, "chan", None, "rows", None),
        P(None, "chan", None, None, None, None),
        P(None, "chan"),
    )
    out_specs = P("chan", "rows", None)
    return jax.shard_map(body, mesh=mesh, in_specs=in_specs, out_specs=out_specs, check_vma=False)
```

```python
import functools
import math

import jax
import jax.numpy as jnp
import ml_dtypes
import numpy as np
from jax import lax
from jax.experimental import pallas as pl
from jax.experimental.pallas import tpu as pltpu
from jax.sharding import PartitionSpec as P

M = 128
LAYERS = 2
N = 64
CG = 16
XR = 16
NY = 4096
NX = N * XR
CX = CG * XR
TILE = 1024
TILES = NY // TILE
CHUNKS = 4
F32 = jnp.float32
BF16 = jnp.bfloat16
MESH = pl.DeviceIdType.MESH


def hops(offset):
    return sum(min(d, 4 - d) for d in offset)


OFFSETS = sorted(
    [(y, x, z) for y in range(4) for x in range(4) for z in range(4)][1:],
    key=lambda offset: -hops(offset),
)


def np_angles(count, freqs, length):
    products = (np.arange(count, dtype=np.int64)[:, None] * freqs[None, :]) % length
    return products.astype(np.float32) * np.float32(2.0 * math.pi / length)


def column_table():
    angles = np_angles(NY, np.arange(M), NY)
    both = np.stack([np.cos(angles), -np.sin(angles)], axis=2).reshape(NY, 2 * M)
    return np.ascontiguousarray(both.T).astype(ml_dtypes.bfloat16)


def row_table():
    j = np.arange(M)
    freqs = np.where(j < M // 2, j, NX - M + j)
    angles = np_angles(NX, freqs, NX)
    cosine = np.cos(angles).astype(ml_dtypes.bfloat16).reshape(N, XR, M).transpose(1, 0, 2)
    sine = np.sin(angles).astype(ml_dtypes.bfloat16).reshape(N, XR, M).transpose(1, 0, 2)
    real = np.concatenate([cosine, -sine], axis=2)
    imag = np.concatenate([sine, cosine], axis=2)
    return np.stack([real, imag], axis=1).reshape(XR * 2 * N, 2 * M)


def dot(a, b):
    return lax.dot_general(a, b, (((1,), (0,)), ((), ())), preferred_element_type=F32)


def dot_nt(a, b):
    return lax.dot_general(a, b, (((1,), (1,)), ((), ())), preferred_element_type=F32)


def gelu(v):
    return 0.5 * v * (1.0 + jnp.tanh(0.7978845608 * (v + 0.044715 * (v * v * v))))


def iota(shape, dim):
    return lax.broadcasted_iota(jnp.int32, shape, dim)


def kernel(
    field,
    table,
    rtable,
    weight,
    taps_any,
    bias_any,
    acc,
    ft,
    spec,
    h,
    rt,
    wt,
    taps,
    bias,
    bias_col,
    hm,
    hp,
    modes,
    snd,
    rcv,
    blk,
    ysc,
    lhs,
    usc,
    vs,
    vr,
    vrow,
    conv_main,
    conv_edge,
    e_snd,
    e_rcv,
    e3,
    ld_sem,
    a_send,
    a_recv,
    c_send,
    c_recv,
    e_send,
    e_recv,
):
    me = lax.axis_index("rows")
    chan = lax.axis_index("chan")
    width = NY // CHUNKS

    loads = []
    for i in range(CHUNKS):
        cols = pl.ds(i * width, width)
        loads.append(
            (
                pltpu.make_async_copy(table.at[:, cols], ft.at[:, cols], ld_sem.at[2 * i]),
                pltpu.make_async_copy(field.at[:, cols], h.at[:, cols], ld_sem.at[2 * i + 1]),
            )
        )
    load_rt = pltpu.make_async_copy(rtable, rt, ld_sem.at[2 * CHUNKS])
    load_wt = pltpu.make_async_copy(weight, wt, ld_sem.at[2 * CHUNKS + 1])
    load_taps = pltpu.make_async_copy(taps_any, taps, ld_sem.at[2 * CHUNKS + 2])
    load_bias = pltpu.make_async_copy(bias_any, bias, ld_sem.at[2 * CHUNKS + 3])
    for one, two in loads:
        one.start()
        two.start()
    load_taps.start()
    load_bias.start()
    load_rt.start()
    load_wt.start()

    barrier = pltpu.get_barrier_semaphore()

    def greet(i, carry):
        pl.semaphore_signal(
            barrier, inc=1, device_id={"rows": lax.rem(me + i, N)}, device_id_type=MESH
        )
        return carry

    lax.fori_loop(1, N, greet, 0)
    pl.semaphore_signal(barrier, inc=1, device_id={"chan": 1 - chan}, device_id_type=MESH)

    ys = [lax.rem(me // 16 + i, 4) * 16 for i in range(4)]
    xs = [lax.rem(me // 4 + i, 4) * 4 for i in range(4)]
    zs = [lax.rem(me + i, 4) for i in range(4)]

    def exchange(index):
        src, dst = snd.at[index], rcv.at[index]
        for y, x, z in OFFSETS:
            d = ys[y] + xs[x] + zs[z]
            pltpu.make_async_remote_copy(
                src_ref=src.at[d],
                dst_ref=dst.at[me],
                send_sem=a_send.at[index],
                recv_sem=a_recv.at[index],
                device_id={"rows": d},
                device_id_type=MESH,
            ).start()
        pltpu.make_async_copy(src.at[me], dst.at[me], a_recv.at[index]).start()

    def exchange_done(index):
        dst = rcv.at[index]
        pltpu.make_async_copy(dst, dst, a_recv.at[index]).wait()

    def edge_copies(layer):
        up = lax.rem(me + 1, N)
        down = lax.rem(me + N - 1, N)
        return [
            pltpu.make_async_remote_copy(
                src_ref=e_snd.at[layer, side],
                dst_ref=e_rcv.at[layer, side],
                send_sem=e_send.at[layer, side],
                recv_sem=e_recv.at[layer, side],
                device_id={"rows": to},
                device_id_type=MESH,
            )
            for side, to in ((0, up), (1, down))
        ]

    def pack_rows():
        shaped = modes[...].reshape(N // 2, 8, CX)
        a, b = shaped[:, :, :128], shaped[:, :, 128:]
        low = iota((N // 2, 8, 128), 1) < 4
        even = jnp.where(low, a, pltpu.roll(b, 4, 1))
        odd = jnp.where(low, pltpu.roll(a, 4, 1), b)
        return even.astype(BF16), odd.astype(BF16)

    def conv_matrices(layer):
        row = iota((CX, CX), 0) & (XR - 1)
        col = iota((CX, CX), 1) & (XR - 1)
        out_of = ((iota((CX, CG), 0) >> 4) == iota((CX, CG), 1)).astype(F32).astype(BF16)
        in_of = ((iota((CG, CX), 1) >> 4) == iota((CG, CX), 0)).astype(F32).astype(BF16)
        xr = iota((CX, CG), 0) & (XR - 1)
        edge = jnp.zeros((CX, 128), F32)
        for s in range(3):
            total = jnp.zeros((CX, CX), F32)
            for r in range(3):
                tap = dot(out_of, taps[layer, r, s])
                total = jnp.where(col == row + (r - 1), dot(tap.astype(BF16), in_of), total)
                if r != 1:
                    side = 0 if r == 0 else 1
                    at = 0 if r == 0 else XR - 1
                    outer = (me == 0) if r == 0 else (me == N - 1)
                    keep = jnp.where(outer, -1, at)
                    offset = s * 32 + side * CG
                    place = (iota((CG, 128), 1) == iota((CG, 128), 0) + offset).astype(F32)
                    part = jnp.where(xr == keep, tap, 0.0).astype(BF16)
                    edge = edge + dot(part, place.astype(BF16))
            conv_main[layer, s] = total.astype(BF16)
        conv_edge[layer] = edge.astype(BF16)
        of = iota((CX, CG), 0) >> 4
        chosen = jnp.where(of == iota((CX, CG), 1), bias[pl.ds(layer, 1), :], 0.0)
        bias_col[layer] = jnp.sum(chosen, axis=1, keepdims=True)

    def edges_out(layer):
        side = iota((32, CX), 0) >> 4
        want = (iota((32, CX), 0) & 15) * XR + jnp.where(side == 0, XR - 1, 0)
        pick = (iota((32, CX), 1) == want).astype(F32).astype(BF16)

        def step(t, carry):
            cols = pl.ds(pl.multiple_of(t * TILE, TILE), TILE)
            rows = dot(pick, h[:, cols]).astype(BF16)
            e_snd[layer, 0, :, cols] = rows[:CG]
            e_snd[layer, 1, :, cols] = rows[CG:]
            return carry

        lax.fori_loop(0, TILES, step, 0, unroll=True)
        for copy in edge_copies(layer):
            copy.start()

    def shifted(block):
        zero = jnp.zeros((block.shape[0], 1), BF16)
        before = jnp.concatenate([zero, block[:, : NY - 1]], axis=1)
        after = jnp.concatenate([block[:, 1:], zero], axis=1)
        return before, after

    def shift_field():
        def step(i, carry):
            rows = pl.ds(pl.multiple_of(i * 16, 16), 16)
            before, after = shifted(h[rows, :])
            hm[rows, :] = before
            hp[rows, :] = after
            return carry

        lax.fori_loop(0, CX // 16, step, 0)

    def convolve(layer):
        for copy in edge_copies(layer):
            copy.wait()
        for side in range(2):
            block = e_rcv[layer, side]
            before, after = shifted(block)
            e3[pl.ds(side * CG, CG), :] = before
            e3[pl.ds(32 + side * CG, CG), :] = block
            e3[pl.ds(64 + side * CG, CG), :] = after
        e3[pl.ds(96, 32), :] = jnp.zeros((32, NY), BF16)

        def step(t, carry):
            cols = pl.ds(pl.multiple_of(t * TILE, TILE), TILE)
            total = dot(conv_main[layer, 0], hm[:, cols])
            total += dot(conv_main[layer, 1], h[:, cols])
            total += dot(conv_main[layer, 2], hp[:, cols])
            total += dot(conv_edge[layer], e3[:, cols])
            acc[:, cols] = total + bias_col[layer]
            return carry

        lax.fori_loop(0, TILES, step, 0, unroll=True)

    def mix(layer):
        blk[...] = rcv[2 * layer].astype(F32).reshape(N * 8, 128)
        for kk in range(2):
            for half in range(2):
                parts = [blk[pl.ds(half * 4 + 2 * kk + p, N, stride=8), :] for p in range(2)]
                ysc[2 * kk + half] = jnp.concatenate(parts, axis=0).T
        for x in range(XR):
            rows = [ysc[i, pl.ds(x, 8, stride=XR), :] for i in range(4)]
            lhs[:, pl.ds(x * 128, 128)] = jnp.concatenate(rows, axis=0).astype(BF16)
        usc[...] = dot(lhs[...], rt[...])
        odd = (iota((8, 128), 0) & 1) == 1
        real = jnp.zeros((8, 8, 128), F32)
        imag = jnp.zeros((8, 8, 128), F32)
        for c in range(CG):
            ur, ui = [
                jnp.where(
                    odd,
                    jnp.broadcast_to(usc[pl.ds(CG + c, 1), pl.ds(p * 128, 128)], (8, 128)),
                    jnp.broadcast_to(usc[pl.ds(c, 1), pl.ds(p * 128, 128)], (8, 128)),
                )[None]
                for p in range(2)
            ]
            wr = wt[layer, 0, c].reshape(8, 8, 128)
            wi = wt[layer, 1, c].reshape(8, 8, 128)
            real += wr * ur - wi * ui
            imag += wr * ui + wi * ur
        vs[layer, :, 0] = real.reshape(2, 32, 128)
        vs[layer, :, 1] = imag.reshape(2, 32, 128)

    def mixed_copy(layer):
        return pltpu.make_async_remote_copy(
            src_ref=vs.at[layer, 1 - chan],
            dst_ref=vr.at[layer],
            send_sem=c_send.at[layer],
            recv_sem=c_recv.at[layer],
            device_id={"chan": 1 - chan},
            device_id_type=MESH,
        )

    def back_rows(layer):
        vrow[...] = vs[layer, chan] + vr[layer]
        mixed = jnp.concatenate(
            [
                jnp.concatenate([vrow[p, pl.ds(kk, CG, stride=2), :] for kk in range(2)], axis=0)
                for p in range(2)
            ],
            axis=1,
        ).astype(BF16)
        for x in range(XR):
            piece = dot_nt(mixed, rt[pl.ds(x * 128, 128), :])
            for i in range(4):
                ysc[i, pl.ds(x, 8, stride=XR), :] = piece[8 * i : 8 * i + 8]
        scale = 2.0 / (M * math.sqrt(NX * NY))
        for kk in range(2):
            first = jnp.where(me == 0, 0.5 * scale, scale) if kk == 0 else scale
            for half in range(2):
                flipped = ysc[2 * kk + half].T * first
                for p in range(2):
                    blk[pl.ds(half * 4 + 2 * kk + p, N, stride=8), :] = flipped[
                        p * N : p * N + N
                    ]
        snd[2 * layer + 1] = blk[...].reshape(N, 8, 128).astype(BF16)

    def spectral_rows(layer):
        wide = rcv[2 * layer + 1].astype(F32).reshape(N // 2, 2, 8, 128)
        even, odd = wide[:, 0], wide[:, 1]
        low = iota((N // 2, 8, 128), 1) < 4
        a = jnp.where(low, even, pltpu.roll(odd, 4, 1)).reshape(CX, 128)
        b = jnp.where(low, pltpu.roll(even, 4, 1), odd).reshape(CX, 128)
        spec[pl.ds(0, 128), :] = a.T.astype(BF16)
        spec[pl.ds(128, 128), :] = b.T.astype(BF16)

    def forward_send(layer):
        even, odd = pack_rows()
        view = snd.at[2 * layer]
        for i in range(N // 2):
            view[2 * i] = even[i]
            view[2 * i + 1] = odd[i]

    modes[...] = jnp.zeros_like(modes)
    for i in range(CHUNKS):
        cols = pl.ds(i * width, width)
        loads[i][0].wait()
        loads[i][1].wait()
        modes[...] += dot_nt(ft[:, cols], h[:, cols])

    for layer in range(LAYERS):
        forward_send(layer)
        if layer == 0:
            pl.semaphore_wait(barrier, N)
        exchange(2 * layer)
        edges_out(layer)
        if layer == 0:
            load_taps.wait()
            load_bias.wait()
            load_rt.wait()
            load_wt.wait()
        shift_field()
        conv_matrices(layer)
        exchange_done(2 * layer)
        mix(layer)
        mixed_copy(layer).start()
        mixed_copy(layer).wait()
        back_rows(layer)
        exchange(2 * layer + 1)
        convolve(layer)
        exchange_done(2 * layer + 1)
        spectral_rows(layer)
        if layer < LAYERS - 1:
            modes[...] = jnp.zeros_like(modes)

            def step(t, carry):
                cols = pl.ds(pl.multiple_of(t * TILE, TILE), TILE)
                value = gelu(acc[:, cols] + dot(spec[...], ft[:, cols])).astype(BF16)
                h[:, cols] = value
                modes[...] += dot_nt(ft[:, cols], value)
                return carry

            lax.fori_loop(0, TILES, step, 0, unroll=True)

    for index in range(2 * LAYERS):
        sent = snd.at[index, pl.ds(0, N - 1)]
        pltpu.make_async_copy(sent, sent, a_send.at[index]).wait()


def finish(acc, ft, spec, out, h, o_sem):
    copies = []
    for t in range(TILES):
        cols = pl.ds(t * TILE, TILE)
        h[:, cols] = gelu(acc[:, cols] + dot(spec[...], ft[:, cols])).astype(BF16)
        copies.append(pltpu.make_async_copy(h.at[:, cols], out.at[:, cols], o_sem.at[t]))
        copies[-1].start()
    for copy in copies:
        copy.wait()


def body(field, spec_weight, conv_weight, bias):
    flat = field.reshape(CX, NY)
    weight = spec_weight.reshape(LAYERS, 2, CG, 64, 128)
    taps = conv_weight.reshape(LAYERS, 3, 3, CG, CG)
    anywhere = pl.BlockSpec(memory_space=pl.ANY)
    operands = [flat, jnp.asarray(column_table()), jnp.asarray(row_table()), weight, taps, bias]
    operands = [pltpu.with_memory_space_constraint(each, pltpu.HBM) for each in operands]
    vmem = pl.BlockSpec(memory_space=pltpu.VMEM)
    acc, ft, spec = pl.pallas_call(
        kernel,
        out_shape=[
            pltpu.VMEM((CX, NY), F32),
            pltpu.VMEM((2 * M, NY), BF16),
            pltpu.VMEM((CX, 2 * M), BF16),
        ],
        in_specs=[anywhere] * 6,
        out_specs=[vmem] * 3,
        scratch_shapes=[
            pltpu.VMEM((CX, NY), BF16),
            pltpu.VMEM((XR * 2 * N, 2 * M), BF16),
            pltpu.VMEM((LAYERS, 2, CG, 64, 128), F32),
            pltpu.VMEM((LAYERS, 3, 3, CG, CG), BF16),
            pltpu.VMEM((LAYERS, CG), F32),
            pltpu.VMEM((LAYERS, CX, 1), F32),
            pltpu.VMEM((CX, NY), BF16),
            pltpu.VMEM((CX, NY), BF16),
            pltpu.VMEM((2 * M, CX), F32),
            pltpu.VMEM((2 * LAYERS, N, 8, 128), BF16),
            pltpu.VMEM((2 * LAYERS, N, 8, 128), BF16),
            pltpu.VMEM((N * 8, 128), F32),
            pltpu.VMEM((4, 128, 128), F32),
            pltpu.VMEM((32, XR * 128), BF16),
            pltpu.VMEM((32, 256), F32),
            pltpu.VMEM((LAYERS, 2, 2, 32, 128), F32),
            pltpu.VMEM((LAYERS, 2, 32, 128), F32),
            pltpu.VMEM((2, 32, 128), F32),
            pltpu.VMEM((LAYERS, 3, CX, CX), BF16),
            pltpu.VMEM((LAYERS, CX, 128), BF16),
            pltpu.VMEM((LAYERS, 2, CG, NY), BF16),
            pltpu.VMEM((LAYERS, 2, CG, NY), BF16),
            pltpu.VMEM((128, NY), BF16),
            pltpu.SemaphoreType.DMA((2 * CHUNKS + 4,)),
            pltpu.SemaphoreType.DMA((2 * LAYERS,)),
            pltpu.SemaphoreType.DMA((2 * LAYERS,)),
            pltpu.SemaphoreType.DMA((LAYERS,)),
            pltpu.SemaphoreType.DMA((LAYERS,)),
            pltpu.SemaphoreType.DMA((LAYERS, 2)),
            pltpu.SemaphoreType.DMA((LAYERS, 2)),
        ],
        compiler_params=pltpu.CompilerParams(
            collective_id=0, has_side_effects=True, vmem_limit_bytes=40 * 2**20
        ),
        cost_estimate=pl.CostEstimate(
            flops=6 * 10**9, bytes_accessed=10 * 2**20, transcendentals=2 * CX * NY
        ),
        name="fourier_layers",
    )(*operands)
    result = pl.pallas_call(
        finish,
        out_shape=jax.ShapeDtypeStruct((CX, NY), BF16),
        in_specs=[vmem] * 3,
        out_specs=anywhere,
        scratch_shapes=[pltpu.VMEM((CX, NY), BF16), pltpu.SemaphoreType.DMA((TILES,))],
        compiler_params=pltpu.CompilerParams(vmem_limit_bytes=16 * 2**20),
        name="last_rows",
    )(acc, ft, spec)
    return result.reshape(CG, XR, NY)


def solution(mesh):
    in_specs = (
        P("chan", "rows", None),
        P(None, None, "chan", None, "rows", None),
        P(None, "chan", None, None, None, None),
        P(None, "chan"),
    )
    out_specs = P("chan", "rows", None)
    return jax.shard_map(body, mesh=mesh, in_specs=in_specs, out_specs=out_specs, check_vma=False)
```

```python
import functools
import math

import jax
import jax.numpy as jnp
import ml_dtypes
import numpy as np
from jax import lax
from jax.experimental import pallas as pl
from jax.experimental.pallas import tpu as pltpu
from jax.sharding import PartitionSpec as P

M = 128
LAYERS = 2
N = 64
CG = 16
XR = 16
NY = 4096
NX = N * XR
CX = CG * XR
TILE = 1024
TILES = NY // TILE
PIECE = 512
PIECES = NY // PIECE
CHUNKS = 4
F32 = jnp.float32
BF16 = jnp.bfloat16
MESH = pl.DeviceIdType.MESH


def hops(offset):
    return sum(min(d, 4 - d) for d in offset)


OFFSETS = sorted(
    [(y, x, z) for y in range(4) for x in range(4) for z in range(4)][1:],
    key=lambda offset: -hops(offset),
)


def np_angles(count, freqs, length):
    products = (np.arange(count, dtype=np.int64)[:, None] * freqs[None, :]) % length
    return products.astype(np.float32) * np.float32(2.0 * math.pi / length)


def column_table():
    angles = np_angles(NY, np.arange(M), NY)
    both = np.stack([np.cos(angles), -np.sin(angles)], axis=2).reshape(NY, 2 * M)
    return np.ascontiguousarray(both.T).astype(ml_dtypes.bfloat16)


def row_table():
    j = np.arange(M)
    freqs = np.where(j < M // 2, j, NX - M + j)
    angles = np_angles(NX, freqs, NX)
    cosine = np.cos(angles).astype(ml_dtypes.bfloat16).reshape(N, XR, M).transpose(1, 0, 2)
    sine = np.sin(angles).astype(ml_dtypes.bfloat16).reshape(N, XR, M).transpose(1, 0, 2)
    real = np.concatenate([cosine, -sine], axis=2)
    imag = np.concatenate([sine, cosine], axis=2)
    return np.stack([real, imag], axis=1).reshape(XR * 2 * N, 2 * M)


def dot(a, b):
    return lax.dot_general(a, b, (((1,), (0,)), ((), ())), preferred_element_type=F32)


def dot_nt(a, b):
    return lax.dot_general(a, b, (((1,), (1,)), ((), ())), preferred_element_type=F32)


def gelu(v):
    half = 0.5 * v
    return half + half * jnp.tanh(v * (0.7978845608 + (0.7978845608 * 0.044715) * (v * v)))


def iota(shape, dim):
    return lax.broadcasted_iota(jnp.int32, shape, dim)


def kernel(
    field,
    table,
    rtable,
    btable,
    weight,
    taps_any,
    bias_any,
    acc,
    ft,
    spec,
    h,
    rt,
    bt,
    wt,
    taps,
    bias,
    bias_col,
    hm,
    hp,
    modes,
    snd,
    rcv,
    blk,
    ysc,
    lhs,
    usc,
    vs,
    vr,
    vrow,
    conv_main,
    conv_edge,
    e_snd,
    e_rcv,
    e3,
    ld_sem,
    a_send,
    a_recv,
    c_send,
    c_recv,
    e_send,
    e_recv,
):
    me = lax.axis_index("rows")
    chan = lax.axis_index("chan")
    width = NY // CHUNKS

    loads = []
    for i in range(CHUNKS):
        cols = pl.ds(i * width, width)
        loads.append(
            (
                pltpu.make_async_copy(table.at[:, cols], ft.at[:, cols], ld_sem.at[2 * i]),
                pltpu.make_async_copy(field.at[:, cols], h.at[:, cols], ld_sem.at[2 * i + 1]),
            )
        )
    load_rt = pltpu.make_async_copy(rtable, rt, ld_sem.at[2 * CHUNKS])
    load_bt = pltpu.make_async_copy(btable, bt, ld_sem.at[2 * CHUNKS + 4])
    load_wt = pltpu.make_async_copy(weight, wt, ld_sem.at[2 * CHUNKS + 1])
    load_taps = pltpu.make_async_copy(taps_any, taps, ld_sem.at[2 * CHUNKS + 2])
    load_bias = pltpu.make_async_copy(bias_any, bias, ld_sem.at[2 * CHUNKS + 3])
    for one, two in loads:
        one.start()
        two.start()
    load_taps.start()
    load_bias.start()
    load_rt.start()
    load_wt.start()
    load_bt.start()

    barrier = pltpu.get_barrier_semaphore()

    def greet(i, carry):
        pl.semaphore_signal(
            barrier, inc=1, device_id={"rows": lax.rem(me + i, N)}, device_id_type=MESH
        )
        return carry

    lax.fori_loop(1, N, greet, 0)
    pl.semaphore_signal(barrier, inc=1, device_id={"chan": 1 - chan}, device_id_type=MESH)

    ys = [lax.rem(me // 16 + i, 4) * 16 for i in range(4)]
    xs = [lax.rem(me // 4 + i, 4) * 4 for i in range(4)]
    zs = [lax.rem(me + i, 4) for i in range(4)]

    def exchange(index):
        src, dst = snd.at[index], rcv.at[index]
        for y, x, z in OFFSETS:
            d = ys[y] + xs[x] + zs[z]
            pltpu.make_async_remote_copy(
                src_ref=src.at[d],
                dst_ref=dst.at[me],
                send_sem=a_send.at[index],
                recv_sem=a_recv.at[index],
                device_id={"rows": d},
                device_id_type=MESH,
            ).start()
        pltpu.make_async_copy(src.at[me], dst.at[me], a_recv.at[index]).start()

    def exchange_done(index):
        dst = rcv.at[index]
        pltpu.make_async_copy(dst, dst, a_recv.at[index]).wait()

    def edge_copies(layer):
        up = lax.rem(me + 1, N)
        down = lax.rem(me + N - 1, N)
        return [
            pltpu.make_async_remote_copy(
                src_ref=e_snd.at[layer, side],
                dst_ref=e_rcv.at[layer, side],
                send_sem=e_send.at[layer, side],
                recv_sem=e_recv.at[layer, side],
                device_id={"rows": to},
                device_id_type=MESH,
            )
            for side, to in ((0, up), (1, down))
        ]

    def pack_rows():
        shaped = modes[...].reshape(N // 2, 8, CX)
        a, b = shaped[:, :, :128], shaped[:, :, 128:]
        low = iota((N // 2, 8, 128), 1) < 4
        even = jnp.where(low, a, pltpu.roll(b, 4, 1))
        odd = jnp.where(low, pltpu.roll(a, 4, 1), b)
        return even.astype(BF16), odd.astype(BF16)

    def conv_matrices(layer):
        row = iota((CX, CX), 0) & (XR - 1)
        col = iota((CX, CX), 1) & (XR - 1)
        out_of = ((iota((CX, CG), 0) >> 4) == iota((CX, CG), 1)).astype(F32).astype(BF16)
        in_of = ((iota((CG, CX), 1) >> 4) == iota((CG, CX), 0)).astype(F32).astype(BF16)
        xr = iota((CX, CG), 0) & (XR - 1)
        edge = jnp.zeros((CX, 128), F32)
        for s in range(3):
            total = jnp.zeros((CX, CX), F32)
            for r in range(3):
                tap = dot(out_of, taps[layer, r, s])
                total = jnp.where(col == row + (r - 1), dot(tap.astype(BF16), in_of), total)
                if r != 1:
                    side = 0 if r == 0 else 1
                    at = 0 if r == 0 else XR - 1
                    outer = (me == 0) if r == 0 else (me == N - 1)
                    keep = jnp.where(outer, -1, at)
                    offset = s * 32 + side * CG
                    place = (iota((CG, 128), 1) == iota((CG, 128), 0) + offset).astype(F32)
                    part = jnp.where(xr == keep, tap, 0.0).astype(BF16)
                    edge = edge + dot(part, place.astype(BF16))
            conv_main[layer, s] = total.astype(BF16)
        conv_edge[layer] = edge.astype(BF16)
        of = iota((CX, CG), 0) >> 4
        chosen = jnp.where(of == iota((CX, CG), 1), bias[pl.ds(layer, 1), :], 0.0)
        bias_col[layer] = jnp.sum(chosen, axis=1, keepdims=True)

    def edges_out(layer):
        side = iota((32, CX), 0) >> 4
        want = (iota((32, CX), 0) & 15) * XR + jnp.where(side == 0, XR - 1, 0)
        pick = (iota((32, CX), 1) == want).astype(F32).astype(BF16)

        def step(t, carry):
            cols = pl.ds(pl.multiple_of(t * TILE, TILE), TILE)
            rows = dot(pick, h[:, cols]).astype(BF16)
            e_snd[layer, 0, :, cols] = rows[:CG]
            e_snd[layer, 1, :, cols] = rows[CG:]
            return carry

        lax.fori_loop(0, TILES, step, 0, unroll=True)
        for copy in edge_copies(layer):
            copy.start()

    def shifted(block):
        zero = jnp.zeros((block.shape[0], 1), BF16)
        before = jnp.concatenate([zero, block[:, : NY - 1]], axis=1)
        after = jnp.concatenate([block[:, 1:], zero], axis=1)
        return before, after

    def shift_field():
        def step(i, carry):
            rows = pl.ds(pl.multiple_of(i * 16, 16), 16)
            before, after = shifted(h[rows, :])
            hm[rows, :] = before
            hp[rows, :] = after
            return carry

        lax.fori_loop(0, CX // 16, step, 0)

    def convolve(layer):
        for copy in edge_copies(layer):
            copy.wait()
        for side in range(2):
            block = e_rcv[layer, side]
            before, after = shifted(block)
            e3[pl.ds(side * CG, CG), :] = before
            e3[pl.ds(32 + side * CG, CG), :] = block
            e3[pl.ds(64 + side * CG, CG), :] = after
        e3[pl.ds(96, 32), :] = jnp.zeros((32, NY), BF16)

        def step(t, carry):
            cols = pl.ds(pl.multiple_of(t * TILE, TILE), TILE)
            total = dot(conv_main[layer, 0], hm[:, cols])
            total += dot(conv_main[layer, 1], h[:, cols])
            total += dot(conv_main[layer, 2], hp[:, cols])
            total += dot(conv_edge[layer], e3[:, cols])
            acc[:, cols] = total + bias_col[layer]
            return carry

        lax.fori_loop(0, TILES, step, 0, unroll=True)

    def mix(layer):
        blk[...] = rcv[2 * layer].astype(F32).reshape(N * 8, 128)
        for kk in range(2):
            for half in range(2):
                parts = [blk[pl.ds(half * 4 + 2 * kk + p, N, stride=8), :] for p in range(2)]
                ysc[2 * kk + half] = jnp.concatenate(parts, axis=0).T
        for x in range(XR):
            rows = [ysc[i, pl.ds(x, 8, stride=XR), :] for i in range(4)]
            lhs[:, pl.ds(x * 128, 128)] = jnp.concatenate(rows, axis=0).astype(BF16)
        usc[...] = dot(lhs[...], rt[...])
        odd = (iota((8, 128), 0) & 1) == 1
        values = []
        for c in range(CG):
            values.append(
                [
                    jnp.where(
                        odd,
                        jnp.broadcast_to(usc[pl.ds(CG + c, 1), pl.ds(p * 128, 128)], (8, 128)),
                        jnp.broadcast_to(usc[pl.ds(c, 1), pl.ds(p * 128, 128)], (8, 128)),
                    )[None]
                    for p in range(2)
                ]
            )

        def half_of(part):
            rows = pl.ds(pl.multiple_of(part * 32, 32), 32)
            real = jnp.zeros((4, 8, 128), F32)
            imag = jnp.zeros((4, 8, 128), F32)
            for c in range(CG):
                ur, ui = values[c]
                wr = wt[layer, 0, c, rows, :].reshape(4, 8, 128)
                wi = wt[layer, 1, c, rows, :].reshape(4, 8, 128)
                real += wr * ur - wi * ui
                imag += wr * ui + wi * ur
            return real.reshape(32, 128), imag.reshape(32, 128)

        vs[layer, 0], vs[layer, 1] = half_of(1 - chan)
        mixed_copy(layer).start()
        vrow[0], vrow[1] = half_of(chan)

    def mixed_copy(layer):
        return pltpu.make_async_remote_copy(
            src_ref=vs.at[layer],
            dst_ref=vr.at[layer],
            send_sem=c_send.at[layer],
            recv_sem=c_recv.at[layer],
            device_id={"chan": 1 - chan},
            device_id_type=MESH,
        )

    def back_rows(layer):
        vrow[...] += vr[layer]
        mixed = jnp.concatenate(
            [
                jnp.concatenate([vrow[p, pl.ds(kk, CG, stride=2), :] for kk in range(2)], axis=0)
                for p in range(2)
            ],
            axis=1,
        ).astype(BF16)
        product = dot(mixed, bt[...])
        for x in range(XR):
            piece = product[:, x * 128 : x * 128 + 128]
            for i in range(4):
                ysc[i, pl.ds(x, 8, stride=XR), :] = piece[8 * i : 8 * i + 8]
        scale = 2.0 / (M * math.sqrt(NX * NY))
        for kk in range(2):
            first = jnp.where(me == 0, 0.5 * scale, scale) if kk == 0 else scale
            for half in range(2):
                flipped = ysc[2 * kk + half].T * first
                for p in range(2):
                    blk[pl.ds(half * 4 + 2 * kk + p, N, stride=8), :] = flipped[
                        p * N : p * N + N
                    ]
        snd[2 * layer + 1] = blk[...].reshape(N, 8, 128).astype(BF16)

    def spectral_rows(layer):
        wide = rcv[2 * layer + 1].astype(F32).reshape(N // 2, 2, 8, 128)
        even, odd = wide[:, 0], wide[:, 1]
        low = iota((N // 2, 8, 128), 1) < 4
        a = jnp.where(low, even, pltpu.roll(odd, 4, 1)).reshape(CX, 128)
        b = jnp.where(low, pltpu.roll(even, 4, 1), odd).reshape(CX, 128)
        spec[pl.ds(0, 128), :] = a.T.astype(BF16)
        spec[pl.ds(128, 128), :] = b.T.astype(BF16)

    def forward_send(layer):
        even, odd = pack_rows()
        view = snd.at[2 * layer]
        for i in range(N // 2):
            view[2 * i] = even[i]
            view[2 * i + 1] = odd[i]

    modes[...] = jnp.zeros_like(modes)
    for i in range(CHUNKS):
        cols = pl.ds(i * width, width)
        loads[i][0].wait()
        loads[i][1].wait()
        modes[...] += dot_nt(ft[:, cols], h[:, cols])

    for layer in range(LAYERS):
        forward_send(layer)
        if layer == 0:
            pl.semaphore_wait(barrier, N)
        exchange(2 * layer)
        edges_out(layer)
        if layer == 0:
            load_taps.wait()
            load_bias.wait()
            load_rt.wait()
            load_wt.wait()
            load_bt.wait()
        shift_field()
        conv_matrices(layer)
        exchange_done(2 * layer)
        mix(layer)
        mixed_copy(layer).wait()
        back_rows(layer)
        exchange(2 * layer + 1)
        convolve(layer)
        exchange_done(2 * layer + 1)
        spectral_rows(layer)
        if layer < LAYERS - 1:
            modes[...] = jnp.zeros_like(modes)

            for t, cols, product in column_pieces(spec, ft):
                value = gelu(acc[:, cols] + product).astype(BF16)
                h[:, cols] = value
                modes[...] += dot_nt(ft[:, cols], value)

    for index in range(2 * LAYERS):
        sent = snd.at[index, pl.ds(0, N - 1)]
        pltpu.make_async_copy(sent, sent, a_send.at[index]).wait()


def column_pieces(spec, ft):
    ahead = dot(spec[...], ft[:, pl.ds(0, PIECE)])
    for t in range(PIECES):
        now = ahead
        if t + 1 < PIECES:
            ahead = dot(spec[...], ft[:, pl.ds((t + 1) * PIECE, PIECE)])
        yield t, pl.ds(t * PIECE, PIECE), now


def finish(acc, ft, spec, out, h, o_sem):
    copies = []
    for t, cols, product in column_pieces(spec, ft):
        h[:, cols] = gelu(acc[:, cols] + product).astype(BF16)
        copies.append(pltpu.make_async_copy(h.at[:, cols], out.at[:, cols], o_sem.at[t]))
        copies[-1].start()
    for copy in copies:
        copy.wait()


def body(field, spec_weight, conv_weight, bias):
    flat = field.reshape(CX, NY)
    weight = spec_weight.reshape(LAYERS, 2, CG, 64, 128)
    taps = conv_weight.reshape(LAYERS, 3, 3, CG, CG)
    anywhere = pl.BlockSpec(memory_space=pl.ANY)
    rows = row_table()
    tables = [jnp.asarray(each) for each in (column_table(), rows, np.ascontiguousarray(rows.T))]
    operands = [flat, *tables, weight, taps, bias]
    operands = [pltpu.with_memory_space_constraint(each, pltpu.HBM) for each in operands]
    vmem = pl.BlockSpec(memory_space=pltpu.VMEM)
    acc, ft, spec = pl.pallas_call(
        kernel,
        out_shape=[
            pltpu.VMEM((CX, NY), F32),
            pltpu.VMEM((2 * M, NY), BF16),
            pltpu.VMEM((CX, 2 * M), BF16),
        ],
        in_specs=[anywhere] * 7,
        out_specs=[vmem] * 3,
        scratch_shapes=[
            pltpu.VMEM((CX, NY), BF16),
            pltpu.VMEM((XR * 2 * N, 2 * M), BF16),
            pltpu.VMEM((2 * M, XR * 2 * N), BF16),
            pltpu.VMEM((LAYERS, 2, CG, 64, 128), F32),
            pltpu.VMEM((LAYERS, 3, 3, CG, CG), BF16),
            pltpu.VMEM((LAYERS, CG), F32),
            pltpu.VMEM((LAYERS, CX, 1), F32),
            pltpu.VMEM((CX, NY), BF16),
            pltpu.VMEM((CX, NY), BF16),
            pltpu.VMEM((2 * M, CX), F32),
            pltpu.VMEM((2 * LAYERS, N, 8, 128), BF16),
            pltpu.VMEM((2 * LAYERS, N, 8, 128), BF16),
            pltpu.VMEM((N * 8, 128), F32),
            pltpu.VMEM((4, 128, 128), F32),
            pltpu.VMEM((32, XR * 128), BF16),
            pltpu.VMEM((32, 256), F32),
            pltpu.VMEM((LAYERS, 2, 32, 128), F32),
            pltpu.VMEM((LAYERS, 2, 32, 128), F32),
            pltpu.VMEM((2, 32, 128), F32),
            pltpu.VMEM((LAYERS, 3, CX, CX), BF16),
            pltpu.VMEM((LAYERS, CX, 128), BF16),
            pltpu.VMEM((LAYERS, 2, CG, NY), BF16),
            pltpu.VMEM((LAYERS, 2, CG, NY), BF16),
            pltpu.VMEM((128, NY), BF16),
            pltpu.SemaphoreType.DMA((2 * CHUNKS + 5,)),
            pltpu.SemaphoreType.DMA((2 * LAYERS,)),
            pltpu.SemaphoreType.DMA((2 * LAYERS,)),
            pltpu.SemaphoreType.DMA((LAYERS,)),
            pltpu.SemaphoreType.DMA((LAYERS,)),
            pltpu.SemaphoreType.DMA((LAYERS, 2)),
            pltpu.SemaphoreType.DMA((LAYERS, 2)),
        ],
        compiler_params=pltpu.CompilerParams(
            collective_id=0, has_side_effects=True, vmem_limit_bytes=40 * 2**20
        ),
        cost_estimate=pl.CostEstimate(
            flops=6 * 10**9, bytes_accessed=10 * 2**20, transcendentals=2 * CX * NY
        ),
        name="fourier_layers",
    )(*operands)
    result = pl.pallas_call(
        finish,
        out_shape=jax.ShapeDtypeStruct((CX, NY), BF16),
        in_specs=[vmem] * 3,
        out_specs=anywhere,
        scratch_shapes=[pltpu.VMEM((CX, NY), BF16), pltpu.SemaphoreType.DMA((PIECES,))],
        compiler_params=pltpu.CompilerParams(vmem_limit_bytes=16 * 2**20),
        name="last_rows",
    )(acc, ft, spec)
    return result.reshape(CG, XR, NY)


def solution(mesh):
    in_specs = (
        P("chan", "rows", None),
        P(None, None, "chan", None, "rows", None),
        P(None, "chan", None, None, None, None),
        P(None, "chan"),
    )
    out_specs = P("chan", "rows", None)
    return jax.shard_map(body, mesh=mesh, in_specs=in_specs, out_specs=out_specs, check_vma=False)
```

```python
import functools
import math

import jax
import jax.numpy as jnp
import ml_dtypes
import numpy as np
from jax import lax
from jax.experimental import pallas as pl
from jax.experimental.pallas import tpu as pltpu
from jax.sharding import PartitionSpec as P

M = 128
LAYERS = 2
N = 64
CG = 16
XR = 16
NY = 4096
NX = N * XR
CX = CG * XR
TILE = 1024
TILES = NY // TILE
PIECE = 512
PIECES = NY // PIECE
CHUNKS = 4
F32 = jnp.float32
BF16 = jnp.bfloat16
MESH = pl.DeviceIdType.MESH


def hops(offset):
    return sum(min(d, 4 - d) for d in offset)


OFFSETS = sorted(
    [(y, x, z) for y in range(4) for x in range(4) for z in range(4)][1:],
    key=lambda offset: -hops(offset),
)


def np_angles(count, freqs, length):
    products = (np.arange(count, dtype=np.int64)[:, None] * freqs[None, :]) % length
    return products.astype(np.float32) * np.float32(2.0 * math.pi / length)


def column_table():
    angles = np_angles(NY, np.arange(M), NY)
    both = np.stack([np.cos(angles), -np.sin(angles)], axis=2).reshape(NY, 2 * M)
    return np.ascontiguousarray(both.T).astype(ml_dtypes.bfloat16)


def row_table():
    j = np.arange(M)
    freqs = np.where(j < M // 2, j, NX - M + j)
    angles = np_angles(NX, freqs, NX)
    cosine = np.cos(angles).astype(ml_dtypes.bfloat16).reshape(N, XR, M).transpose(1, 0, 2)
    sine = np.sin(angles).astype(ml_dtypes.bfloat16).reshape(N, XR, M).transpose(1, 0, 2)
    real = np.concatenate([cosine, -sine], axis=2)
    imag = np.concatenate([sine, cosine], axis=2)
    return np.stack([real, imag], axis=1).reshape(XR * 2 * N, 2 * M)


def dot(a, b):
    return lax.dot_general(a, b, (((1,), (0,)), ((), ())), preferred_element_type=F32)


def dot_nt(a, b):
    return lax.dot_general(a, b, (((1,), (1,)), ((), ())), preferred_element_type=F32)


def gelu_of_half(w):
    inner = w * (2.0 * 0.7978845608 + (8.0 * 0.7978845608 * 0.044715) * (w * w))
    return w + w * jnp.tanh(inner)


def iota(shape, dim):
    return lax.broadcasted_iota(jnp.int32, shape, dim)


def kernel(
    field,
    table,
    rtable,
    btable,
    weight,
    taps_any,
    bias_any,
    acc,
    ft,
    spec,
    h,
    rt,
    bt,
    wt,
    taps,
    bias,
    bias_col,
    hm,
    hp,
    modes,
    snd,
    rcv,
    blk,
    ysc,
    lhs,
    usc,
    vs,
    vr,
    vrow,
    conv_main,
    conv_edge,
    e_snd,
    e_rcv,
    e3,
    ld_sem,
    a_send,
    a_recv,
    c_send,
    c_recv,
    e_send,
    e_recv,
):
    me = lax.axis_index("rows")
    chan = lax.axis_index("chan")
    width = NY // CHUNKS
    barrier = pltpu.get_barrier_semaphore()
    ys = [lax.rem(me // 16 + i, 4) * 16 for i in range(4)]
    xs = [lax.rem(me // 4 + i, 4) * 4 for i in range(4)]
    zs = [lax.rem(me + i, 4) for i in range(4)]

    def greet(offsets):
        for y, x, z in offsets:
            pl.semaphore_signal(
                barrier, inc=1, device_id={"rows": ys[y] + xs[x] + zs[z]}, device_id_type=MESH
            )

    greet(OFFSETS[:7])

    loads = []
    for i in range(CHUNKS):
        cols = pl.ds(i * width, width)
        loads.append(
            (
                pltpu.make_async_copy(table.at[:, cols], ft.at[:, cols], ld_sem.at[2 * i]),
                pltpu.make_async_copy(field.at[:, cols], h.at[:, cols], ld_sem.at[2 * i + 1]),
            )
        )
    load_rt = pltpu.make_async_copy(rtable, rt, ld_sem.at[2 * CHUNKS])
    load_bt = pltpu.make_async_copy(btable, bt, ld_sem.at[2 * CHUNKS + 4])
    load_wt = pltpu.make_async_copy(weight, wt, ld_sem.at[2 * CHUNKS + 1])
    load_taps = pltpu.make_async_copy(taps_any, taps, ld_sem.at[2 * CHUNKS + 2])
    load_bias = pltpu.make_async_copy(bias_any, bias, ld_sem.at[2 * CHUNKS + 3])
    for one, two in loads:
        one.start()
        two.start()
    greet(OFFSETS[7:])
    pl.semaphore_signal(barrier, inc=1, device_id={"chan": 1 - chan}, device_id_type=MESH)
    load_taps.start()
    load_bias.start()
    load_rt.start()
    load_wt.start()
    load_bt.start()


    def exchange(index):
        src, dst = snd.at[index], rcv.at[index]
        for y, x, z in OFFSETS:
            d = ys[y] + xs[x] + zs[z]
            pltpu.make_async_remote_copy(
                src_ref=src.at[d],
                dst_ref=dst.at[me],
                send_sem=a_send.at[index],
                recv_sem=a_recv.at[index],
                device_id={"rows": d},
                device_id_type=MESH,
            ).start()
        pltpu.make_async_copy(src.at[me], dst.at[me], a_recv.at[index]).start()

    def exchange_done(index):
        dst = rcv.at[index]
        pltpu.make_async_copy(dst, dst, a_recv.at[index]).wait()

    def edge_copies(layer):
        up = lax.rem(me + 1, N)
        down = lax.rem(me + N - 1, N)
        return [
            pltpu.make_async_remote_copy(
                src_ref=e_snd.at[layer, side],
                dst_ref=e_rcv.at[layer, side],
                send_sem=e_send.at[layer, side],
                recv_sem=e_recv.at[layer, side],
                device_id={"rows": to},
                device_id_type=MESH,
            )
            for side, to in ((0, up), (1, down))
        ]

    def pack_rows():
        shaped = modes[...].reshape(N // 2, 8, CX)
        a, b = shaped[:, :, :128], shaped[:, :, 128:]
        low = iota((N // 2, 8, 128), 1) < 4
        even = jnp.where(low, a, pltpu.roll(b, 4, 1))
        odd = jnp.where(low, pltpu.roll(a, 4, 1), b)
        return even.astype(BF16), odd.astype(BF16)

    def conv_matrices(layer):
        row = iota((CX, CX), 0) & (XR - 1)
        col = iota((CX, CX), 1) & (XR - 1)
        out_of = ((iota((CX, CG), 0) >> 4) == iota((CX, CG), 1)).astype(F32).astype(BF16)
        in_of = ((iota((CG, CX), 1) >> 4) == iota((CG, CX), 0)).astype(F32).astype(BF16)
        xr = iota((CX, CG), 0) & (XR - 1)
        edge = jnp.zeros((CX, 128), F32)
        for s in range(3):
            total = jnp.zeros((CX, CX), F32)
            for r in range(3):
                tap = dot(out_of, taps[layer, r, s])
                total = jnp.where(col == row + (r - 1), dot(tap.astype(BF16), in_of), total)
                if r != 1:
                    side = 0 if r == 0 else 1
                    at = 0 if r == 0 else XR - 1
                    outer = (me == 0) if r == 0 else (me == N - 1)
                    keep = jnp.where(outer, -1, at)
                    offset = s * 32 + side * CG
                    place = (iota((CG, 128), 1) == iota((CG, 128), 0) + offset).astype(F32)
                    part = jnp.where(xr == keep, tap, 0.0).astype(BF16)
                    edge = edge + dot(part, place.astype(BF16))
            conv_main[layer, s] = (0.5 * total).astype(BF16)
        conv_edge[layer] = (0.5 * edge).astype(BF16)
        of = iota((CX, CG), 0) >> 4
        chosen = jnp.where(of == iota((CX, CG), 1), bias[pl.ds(layer, 1), :], 0.0)
        bias_col[layer] = 0.5 * jnp.sum(chosen, axis=1, keepdims=True)

    def edges_out(layer):
        side = iota((32, CX), 0) >> 4
        want = (iota((32, CX), 0) & 15) * XR + jnp.where(side == 0, XR - 1, 0)
        pick = (iota((32, CX), 1) == want).astype(F32).astype(BF16)

        def step(t, carry):
            cols = pl.ds(pl.multiple_of(t * TILE, TILE), TILE)
            rows = dot(pick, h[:, cols]).astype(BF16)
            e_snd[layer, 0, :, cols] = rows[:CG]
            e_snd[layer, 1, :, cols] = rows[CG:]
            return carry

        lax.fori_loop(0, TILES, step, 0, unroll=True)
        for copy in edge_copies(layer):
            copy.start()

    def shifted(block):
        zero = jnp.zeros((block.shape[0], 1), BF16)
        before = jnp.concatenate([zero, block[:, : NY - 1]], axis=1)
        after = jnp.concatenate([block[:, 1:], zero], axis=1)
        return before, after

    def shift_field():
        def step(i, carry):
            rows = pl.ds(pl.multiple_of(i * 16, 16), 16)
            before, after = shifted(h[rows, :])
            hm[rows, :] = before
            hp[rows, :] = after
            return carry

        lax.fori_loop(0, CX // 16, step, 0)

    def edges_in(layer):
        for copy in edge_copies(layer):
            copy.wait()
        for side in range(2):
            block = e_rcv[layer, side]
            before, after = shifted(block)
            e3[pl.ds(side * CG, CG), :] = before
            e3[pl.ds(32 + side * CG, CG), :] = block
            e3[pl.ds(64 + side * CG, CG), :] = after
        e3[pl.ds(96, 32), :] = jnp.zeros((32, NY), BF16)

    def convolve(layer, tiles, main=True, edge=True):
        for t in tiles:
            cols = pl.ds(t * TILE, TILE)
            total = bias_col[layer] if main else acc[:, cols]
            if main:
                total = total + dot(conv_main[layer, 0], hm[:, cols])
                total += dot(conv_main[layer, 1], h[:, cols])
                total += dot(conv_main[layer, 2], hp[:, cols])
            if edge:
                total += dot(conv_edge[layer], e3[:, cols])
            acc[:, cols] = total

    def mix(layer):
        blk[...] = rcv[2 * layer].astype(F32).reshape(N * 8, 128)
        for kk in range(2):
            for half in range(2):
                parts = [blk[pl.ds(half * 4 + 2 * kk + p, N, stride=8), :] for p in range(2)]
                ysc[2 * kk + half] = jnp.concatenate(parts, axis=0).T
        for x in range(XR):
            rows = [ysc[i, pl.ds(x, 8, stride=XR), :] for i in range(4)]
            lhs[:, pl.ds(x * 128, 128)] = jnp.concatenate(rows, axis=0).astype(BF16)
        usc[...] = dot(lhs[...], rt[...])
        odd = (iota((8, 128), 0) & 1) == 1
        values = []
        for c in range(CG):
            values.append(
                [
                    jnp.where(
                        odd,
                        jnp.broadcast_to(usc[pl.ds(CG + c, 1), pl.ds(p * 128, 128)], (8, 128)),
                        jnp.broadcast_to(usc[pl.ds(c, 1), pl.ds(p * 128, 128)], (8, 128)),
                    )[None]
                    for p in range(2)
                ]
            )

        def half_of(part):
            rows = pl.ds(pl.multiple_of(part * 32, 32), 32)
            real = jnp.zeros((4, 8, 128), F32)
            imag = jnp.zeros((4, 8, 128), F32)
            for c in range(CG):
                ur, ui = values[c]
                wr = wt[layer, 0, c, rows, :].reshape(4, 8, 128)
                wi = wt[layer, 1, c, rows, :].reshape(4, 8, 128)
                real += wr * ur - wi * ui
                imag += wr * ui + wi * ur
            return real.reshape(32, 128), imag.reshape(32, 128)

        vs[layer, 0], vs[layer, 1] = half_of(1 - chan)
        mixed_copy(layer).start()
        vrow[0], vrow[1] = half_of(chan)

    def mixed_copy(layer):
        return pltpu.make_async_remote_copy(
            src_ref=vs.at[layer],
            dst_ref=vr.at[layer],
            send_sem=c_send.at[layer],
            recv_sem=c_recv.at[layer],
            device_id={"chan": 1 - chan},
            device_id_type=MESH,
        )

    def back_rows(layer):
        vrow[...] += vr[layer]
        mixed = jnp.concatenate(
            [
                jnp.concatenate([vrow[p, pl.ds(kk, CG, stride=2), :] for kk in range(2)], axis=0)
                for p in range(2)
            ],
            axis=1,
        ).astype(BF16)
        product = dot(mixed, bt[...])
        for x in range(XR):
            piece = product[:, x * 128 : x * 128 + 128]
            for i in range(4):
                ysc[i, pl.ds(x, 8, stride=XR), :] = piece[8 * i : 8 * i + 8]
        scale = 1.0 / (M * math.sqrt(NX * NY))
        for kk in range(2):
            first = jnp.where(me == 0, 0.5 * scale, scale) if kk == 0 else scale
            for half in range(2):
                flipped = ysc[2 * kk + half].T * first
                for p in range(2):
                    blk[pl.ds(half * 4 + 2 * kk + p, N, stride=8), :] = flipped[
                        p * N : p * N + N
                    ]
        snd[2 * layer + 1] = blk[...].reshape(N, 8, 128).astype(BF16)

    def spectral_rows(layer):
        wide = rcv[2 * layer + 1].astype(F32).reshape(N // 2, 2, 8, 128)
        even, odd = wide[:, 0], wide[:, 1]
        low = iota((N // 2, 8, 128), 1) < 4
        a = jnp.where(low, even, pltpu.roll(odd, 4, 1)).reshape(CX, 128)
        b = jnp.where(low, pltpu.roll(even, 4, 1), odd).reshape(CX, 128)
        spec[pl.ds(0, 128), :] = a.T.astype(BF16)
        spec[pl.ds(128, 128), :] = b.T.astype(BF16)

    def forward_send(layer):
        even, odd = pack_rows()
        view = snd.at[2 * layer]
        for i in range(N // 2):
            view[2 * i] = even[i]
            view[2 * i + 1] = odd[i]

    modes[...] = jnp.zeros_like(modes)
    for i in range(CHUNKS):
        cols = pl.ds(i * width, width)
        loads[i][0].wait()
        loads[i][1].wait()
        modes[...] += dot_nt(ft[:, cols], h[:, cols])

    for layer in range(LAYERS):
        forward_send(layer)
        if layer == 0:
            load_taps.wait()
            load_bias.wait()
            conv_matrices(0)
            pl.semaphore_wait(barrier, N)
        exchange(2 * layer)
        edges_out(layer)
        if layer == 0:
            load_rt.wait()
            load_wt.wait()
            load_bt.wait()
        shift_field()
        if layer == 0:
            conv_matrices(1)
        convolve(layer, range(1), edge=False)
        exchange_done(2 * layer)
        mix(layer)
        mixed_copy(layer).wait()
        back_rows(layer)
        exchange(2 * layer + 1)
        edges_in(layer)
        convolve(layer, range(1), main=False)
        convolve(layer, range(1, TILES))
        exchange_done(2 * layer + 1)
        spectral_rows(layer)
        if layer < LAYERS - 1:
            modes[...] = jnp.zeros_like(modes)

            for t, cols, product in column_pieces(spec, ft):
                value = gelu_of_half(acc[:, cols] + product).astype(BF16)
                h[:, cols] = value
                modes[...] += dot_nt(ft[:, cols], value)

    for index in range(2 * LAYERS):
        sent = snd.at[index, pl.ds(0, N - 1)]
        pltpu.make_async_copy(sent, sent, a_send.at[index]).wait()


def column_pieces(spec, ft):
    ahead = dot(spec[...], ft[:, pl.ds(0, PIECE)])
    for t in range(PIECES):
        now = ahead
        if t + 1 < PIECES:
            ahead = dot(spec[...], ft[:, pl.ds((t + 1) * PIECE, PIECE)])
        yield t, pl.ds(t * PIECE, PIECE), now


def finish(acc, ft, spec, out, h, o_sem):
    copies = []
    for t, cols, product in column_pieces(spec, ft):
        h[:, cols] = gelu_of_half(acc[:, cols] + product).astype(BF16)
        copies.append(pltpu.make_async_copy(h.at[:, cols], out.at[:, cols], o_sem.at[t]))
        copies[-1].start()
    for copy in copies:
        copy.wait()


def body(field, spec_weight, conv_weight, bias):
    flat = field.reshape(CX, NY)
    weight = spec_weight.reshape(LAYERS, 2, CG, 64, 128)
    taps = conv_weight.reshape(LAYERS, 3, 3, CG, CG)
    anywhere = pl.BlockSpec(memory_space=pl.ANY)
    rows = row_table()
    tables = [jnp.asarray(each) for each in (column_table(), rows, np.ascontiguousarray(rows.T))]
    operands = [flat, *tables, weight, taps, bias]
    operands = [pltpu.with_memory_space_constraint(each, pltpu.HBM) for each in operands]
    vmem = pl.BlockSpec(memory_space=pltpu.VMEM)
    acc, ft, spec = pl.pallas_call(
        kernel,
        out_shape=[
            pltpu.VMEM((CX, NY), F32),
            pltpu.VMEM((2 * M, NY), BF16),
            pltpu.VMEM((CX, 2 * M), BF16),
        ],
        in_specs=[anywhere] * 7,
        out_specs=[vmem] * 3,
        scratch_shapes=[
            pltpu.VMEM((CX, NY), BF16),
            pltpu.VMEM((XR * 2 * N, 2 * M), BF16),
            pltpu.VMEM((2 * M, XR * 2 * N), BF16),
            pltpu.VMEM((LAYERS, 2, CG, 64, 128), F32),
            pltpu.VMEM((LAYERS, 3, 3, CG, CG), BF16),
            pltpu.VMEM((LAYERS, CG), F32),
            pltpu.VMEM((LAYERS, CX, 1), F32),
            pltpu.VMEM((CX, NY), BF16),
            pltpu.VMEM((CX, NY), BF16),
            pltpu.VMEM((2 * M, CX), F32),
            pltpu.VMEM((2 * LAYERS, N, 8, 128), BF16),
            pltpu.VMEM((2 * LAYERS, N, 8, 128), BF16),
            pltpu.VMEM((N * 8, 128), F32),
            pltpu.VMEM((4, 128, 128), F32),
            pltpu.VMEM((32, XR * 128), BF16),
            pltpu.VMEM((32, 256), F32),
            pltpu.VMEM((LAYERS, 2, 32, 128), F32),
            pltpu.VMEM((LAYERS, 2, 32, 128), F32),
            pltpu.VMEM((2, 32, 128), F32),
            pltpu.VMEM((LAYERS, 3, CX, CX), BF16),
            pltpu.VMEM((LAYERS, CX, 128), BF16),
            pltpu.VMEM((LAYERS, 2, CG, NY), BF16),
            pltpu.VMEM((LAYERS, 2, CG, NY), BF16),
            pltpu.VMEM((128, NY), BF16),
            pltpu.SemaphoreType.DMA((2 * CHUNKS + 5,)),
            pltpu.SemaphoreType.DMA((2 * LAYERS,)),
            pltpu.SemaphoreType.DMA((2 * LAYERS,)),
            pltpu.SemaphoreType.DMA((LAYERS,)),
            pltpu.SemaphoreType.DMA((LAYERS,)),
            pltpu.SemaphoreType.DMA((LAYERS, 2)),
            pltpu.SemaphoreType.DMA((LAYERS, 2)),
        ],
        compiler_params=pltpu.CompilerParams(
            collective_id=0, has_side_effects=True, vmem_limit_bytes=40 * 2**20
        ),
        cost_estimate=pl.CostEstimate(
            flops=6 * 10**9, bytes_accessed=10 * 2**20, transcendentals=2 * CX * NY
        ),
        name="fourier_layers",
    )(*operands)
    result = pl.pallas_call(
        finish,
        out_shape=jax.ShapeDtypeStruct((CX, NY), BF16),
        in_specs=[vmem] * 3,
        out_specs=anywhere,
        scratch_shapes=[pltpu.VMEM((CX, NY), BF16), pltpu.SemaphoreType.DMA((PIECES,))],
        compiler_params=pltpu.CompilerParams(vmem_limit_bytes=16 * 2**20),
        name="last_rows",
    )(acc, ft, spec)
    return result.reshape(CG, XR, NY)


def solution(mesh):
    in_specs = (
        P("chan", "rows", None),
        P(None, None, "chan", None, "rows", None),
        P(None, "chan", None, None, None, None),
        P(None, "chan"),
    )
    out_specs = P("chan", "rows", None)
    return jax.shard_map(body, mesh=mesh, in_specs=in_specs, out_specs=out_specs, check_vma=False)
```

```python
import functools
import math

import jax
import jax.numpy as jnp
import ml_dtypes
import numpy as np
from jax import lax
from jax.experimental import pallas as pl
from jax.experimental.pallas import tpu as pltpu
from jax.sharding import PartitionSpec as P

M = 128
LAYERS = 2
N = 64
CG = 16
XR = 16
NY = 4096
NX = N * XR
CX = CG * XR
TILE = 1024
TILES = NY // TILE
PIECE = 512
PIECES = NY // PIECE
CHUNKS = 4
F32 = jnp.float32
BF16 = jnp.bfloat16
MESH = pl.DeviceIdType.MESH


def hops(offset):
    return sum(min(d, 4 - d) for d in offset)


OFFSETS = sorted(
    [(y, x, z) for y in range(4) for x in range(4) for z in range(4)][1:],
    key=lambda offset: -hops(offset),
)


def np_angles(count, freqs, length):
    products = (np.arange(count, dtype=np.int64)[:, None] * freqs[None, :]) % length
    return products.astype(np.float32) * np.float32(2.0 * math.pi / length)


def column_table():
    angles = np_angles(NY, np.arange(M), NY)
    both = np.stack([np.cos(angles), -np.sin(angles)], axis=2).reshape(NY, 2 * M)
    return np.ascontiguousarray(both.T).astype(ml_dtypes.bfloat16)


def row_table():
    j = np.arange(M)
    freqs = np.where(j < M // 2, j, NX - M + j)
    angles = np_angles(NX, freqs, NX)
    cosine = np.cos(angles).astype(ml_dtypes.bfloat16).reshape(N, XR, M).transpose(1, 0, 2)
    sine = np.sin(angles).astype(ml_dtypes.bfloat16).reshape(N, XR, M).transpose(1, 0, 2)
    real = np.concatenate([cosine, -sine], axis=2)
    imag = np.concatenate([sine, cosine], axis=2)
    return np.stack([real, imag], axis=1).reshape(XR * 2 * N, 2 * M)


def dot(a, b):
    return lax.dot_general(a, b, (((1,), (0,)), ((), ())), preferred_element_type=F32)


def dot_nt(a, b):
    return lax.dot_general(a, b, (((1,), (1,)), ((), ())), preferred_element_type=F32)


def gelu_of_half(w):
    inner = w * (2.0 * 0.7978845608 + (8.0 * 0.7978845608 * 0.044715) * (w * w))
    return w + w * jnp.tanh(inner)


def iota(shape, dim):
    return lax.broadcasted_iota(jnp.int32, shape, dim)


def kernel(
    field,
    table,
    rtable,
    btable,
    weight,
    taps_any,
    bias_any,
    acc,
    ft,
    spec,
    h,
    rt,
    bt,
    wt,
    taps,
    bias,
    bias_col,
    hm,
    hp,
    modes,
    snd,
    rcv,
    blk,
    ysc,
    lhs,
    usc,
    vs,
    vr,
    vrow,
    conv_main,
    conv_edge,
    e_snd,
    e_rcv,
    e3,
    ld_sem,
    a_send,
    a_recv,
    c_send,
    c_recv,
    e_send,
    e_recv,
):
    me = lax.axis_index("rows")
    chan = lax.axis_index("chan")
    width = NY // CHUNKS
    barrier = pltpu.get_barrier_semaphore()
    ys = [lax.rem(me // 16 + i, 4) * 16 for i in range(4)]
    xs = [lax.rem(me // 4 + i, 4) * 4 for i in range(4)]
    zs = [lax.rem(me + i, 4) for i in range(4)]

    def greet(offsets):
        for y, x, z in offsets:
            pl.semaphore_signal(
                barrier, inc=1, device_id={"rows": ys[y] + xs[x] + zs[z]}, device_id_type=MESH
            )

    greet(OFFSETS[:7])

    loads = []
    for i in range(CHUNKS):
        cols = pl.ds(i * width, width)
        loads.append(
            (
                pltpu.make_async_copy(table.at[:, cols], ft.at[:, cols], ld_sem.at[2 * i]),
                pltpu.make_async_copy(field.at[:, cols], h.at[:, cols], ld_sem.at[2 * i + 1]),
            )
        )
    load_rt = pltpu.make_async_copy(rtable, rt, ld_sem.at[2 * CHUNKS])
    load_bt = pltpu.make_async_copy(btable, bt, ld_sem.at[2 * CHUNKS + 4])
    load_wt = pltpu.make_async_copy(weight, wt, ld_sem.at[2 * CHUNKS + 1])
    load_taps = pltpu.make_async_copy(taps_any, taps, ld_sem.at[2 * CHUNKS + 2])
    load_bias = pltpu.make_async_copy(bias_any, bias, ld_sem.at[2 * CHUNKS + 3])
    for one, two in loads:
        one.start()
        two.start()
    greet(OFFSETS[7:])
    pl.semaphore_signal(barrier, inc=1, device_id={"chan": 1 - chan}, device_id_type=MESH)
    load_taps.start()
    load_bias.start()
    load_rt.start()
    load_wt.start()
    load_bt.start()


    def exchange(index):
        src, dst = snd.at[index], rcv.at[index]
        for y, x, z in OFFSETS:
            d = ys[y] + xs[x] + zs[z]
            pltpu.make_async_remote_copy(
                src_ref=src.at[d],
                dst_ref=dst.at[me],
                send_sem=a_send.at[index],
                recv_sem=a_recv.at[index],
                device_id={"rows": d},
                device_id_type=MESH,
            ).start()
        pltpu.make_async_copy(src.at[me], dst.at[me], a_recv.at[index]).start()

    def exchange_done(index):
        dst = rcv.at[index]
        pltpu.make_async_copy(dst, dst, a_recv.at[index]).wait()

    def edge_copies(layer):
        up = lax.rem(me + 1, N)
        down = lax.rem(me + N - 1, N)
        return [
            pltpu.make_async_remote_copy(
                src_ref=e_snd.at[layer, side],
                dst_ref=e_rcv.at[layer, side],
                send_sem=e_send.at[layer, side],
                recv_sem=e_recv.at[layer, side],
                device_id={"rows": to},
                device_id_type=MESH,
            )
            for side, to in ((0, up), (1, down))
        ]

    def pack_rows():
        shaped = modes[...].reshape(N // 2, 8, CX)
        a, b = shaped[:, :, :128], shaped[:, :, 128:]
        low = iota((N // 2, 8, 128), 1) < 4
        even = jnp.where(low, a, pltpu.roll(b, 4, 1))
        odd = jnp.where(low, pltpu.roll(a, 4, 1), b)
        return even.astype(BF16), odd.astype(BF16)

    def conv_matrices(layer):
        row = iota((CX, CX), 0) & (XR - 1)
        col = iota((CX, CX), 1) & (XR - 1)
        out_of = ((iota((CX, CG), 0) >> 4) == iota((CX, CG), 1)).astype(F32).astype(BF16)
        in_of = ((iota((CG, CX), 1) >> 4) == iota((CG, CX), 0)).astype(F32).astype(BF16)
        xr = iota((CX, CG), 0) & (XR - 1)
        edge = jnp.zeros((CX, 128), F32)
        for s in range(3):
            total = jnp.zeros((CX, CX), F32)
            for r in range(3):
                tap = dot(out_of, taps[layer, r, s])
                total = jnp.where(col == row + (r - 1), dot(tap.astype(BF16), in_of), total)
                if r != 1:
                    side = 0 if r == 0 else 1
                    at = 0 if r == 0 else XR - 1
                    outer = (me == 0) if r == 0 else (me == N - 1)
                    keep = jnp.where(outer, -1, at)
                    offset = s * 32 + side * CG
                    place = (iota((CG, 128), 1) == iota((CG, 128), 0) + offset).astype(F32)
                    part = jnp.where(xr == keep, tap, 0.0).astype(BF16)
                    edge = edge + dot(part, place.astype(BF16))
            conv_main[layer, s] = (0.5 * total).astype(BF16)
        conv_edge[layer] = (0.5 * edge).astype(BF16)
        of = iota((CX, CG), 0) >> 4
        chosen = jnp.where(of == iota((CX, CG), 1), bias[pl.ds(layer, 1), :], 0.0)
        bias_col[layer] = 0.5 * jnp.sum(chosen, axis=1, keepdims=True)

    def edges_out(layer):
        side = iota((32, CX), 0) >> 4
        want = (iota((32, CX), 0) & 15) * XR + jnp.where(side == 0, XR - 1, 0)
        pick = (iota((32, CX), 1) == want).astype(F32).astype(BF16)

        def step(t, carry):
            cols = pl.ds(pl.multiple_of(t * TILE, TILE), TILE)
            rows = dot(pick, h[:, cols]).astype(BF16)
            e_snd[layer, 0, :, cols] = rows[:CG]
            e_snd[layer, 1, :, cols] = rows[CG:]
            return carry

        lax.fori_loop(0, TILES, step, 0, unroll=True)
        for copy in edge_copies(layer):
            copy.start()

    def shifted(block):
        zero = jnp.zeros((block.shape[0], 1), BF16)
        before = jnp.concatenate([zero, block[:, : NY - 1]], axis=1)
        after = jnp.concatenate([block[:, 1:], zero], axis=1)
        return before, after

    def shift_field():
        def step(i, carry):
            rows = pl.ds(pl.multiple_of(i * 16, 16), 16)
            before, after = shifted(h[rows, :])
            hm[rows, :] = before
            hp[rows, :] = after
            return carry

        lax.fori_loop(0, CX // 16, step, 0)

    def edges_in(layer):
        for copy in edge_copies(layer):
            copy.wait()
        for side in range(2):
            block = e_rcv[layer, side]
            before, after = shifted(block)
            e3[pl.ds(side * CG, CG), :] = before
            e3[pl.ds(32 + side * CG, CG), :] = block
            e3[pl.ds(64 + side * CG, CG), :] = after
        e3[pl.ds(96, 32), :] = jnp.zeros((32, NY), BF16)

    def convolve(layer, tiles, main=True, edge=True):
        for t in tiles:
            cols = pl.ds(t * TILE, TILE)
            total = bias_col[layer] if main else acc[:, cols]
            if main:
                total = total + dot(conv_main[layer, 0], hm[:, cols])
                total += dot(conv_main[layer, 1], h[:, cols])
                total += dot(conv_main[layer, 2], hp[:, cols])
            if edge:
                total += dot(conv_edge[layer], e3[:, cols])
            acc[:, cols] = total

    def mix(layer):
        blk[...] = rcv[2 * layer].astype(F32).reshape(N * 8, 128)
        for kk in range(2):
            for half in range(2):
                parts = [blk[pl.ds(half * 4 + 2 * kk + p, N, stride=8), :] for p in range(2)]
                ysc[2 * kk + half] = jnp.concatenate(parts, axis=0).T
        for x in range(XR):
            rows = [ysc[i, pl.ds(x, 8, stride=XR), :] for i in range(4)]
            lhs[:, pl.ds(x * 128, 128)] = jnp.concatenate(rows, axis=0).astype(BF16)
        usc[...] = dot(lhs[...], rt[...])
        odd = (iota((8, 128), 0) & 1) == 1
        values = []
        for c in range(CG):
            values.append(
                [
                    jnp.where(
                        odd,
                        jnp.broadcast_to(usc[pl.ds(CG + c, 1), pl.ds(p * 128, 128)], (8, 128)),
                        jnp.broadcast_to(usc[pl.ds(c, 1), pl.ds(p * 128, 128)], (8, 128)),
                    )[None]
                    for p in range(2)
                ]
            )

        def half_of(part):
            rows = pl.ds(pl.multiple_of(part * 32, 32), 32)
            real = jnp.zeros((4, 8, 128), F32)
            imag = jnp.zeros((4, 8, 128), F32)
            for c in range(CG):
                ur, ui = values[c]
                wr = wt[layer, 0, c, rows, :].reshape(4, 8, 128)
                wi = wt[layer, 1, c, rows, :].reshape(4, 8, 128)
                real += wr * ur - wi * ui
                imag += wr * ui + wi * ur
            return real.reshape(32, 128), imag.reshape(32, 128)

        vs[layer, 0], vs[layer, 1] = half_of(1 - chan)
        mixed_copy(layer).start()
        vrow[0], vrow[1] = half_of(chan)

    def mixed_copy(layer):
        return pltpu.make_async_remote_copy(
            src_ref=vs.at[layer],
            dst_ref=vr.at[layer],
            send_sem=c_send.at[layer],
            recv_sem=c_recv.at[layer],
            device_id={"chan": 1 - chan},
            device_id_type=MESH,
        )

    def back_rows(layer):
        vrow[...] += vr[layer]
        mixed = jnp.concatenate(
            [
                jnp.concatenate([vrow[p, pl.ds(kk, CG, stride=2), :] for kk in range(2)], axis=0)
                for p in range(2)
            ],
            axis=1,
        ).astype(BF16)
        product = dot(mixed, bt[...])
        for x in range(XR):
            piece = product[:, x * 128 : x * 128 + 128]
            for i in range(4):
                ysc[i, pl.ds(x, 8, stride=XR), :] = piece[8 * i : 8 * i + 8]
        scale = 1.0 / (M * math.sqrt(NX * NY))
        for kk in range(2):
            first = jnp.where(me == 0, 0.5 * scale, scale) if kk == 0 else scale
            for half in range(2):
                flipped = ysc[2 * kk + half].T * first
                for p in range(2):
                    blk[pl.ds(half * 4 + 2 * kk + p, N, stride=8), :] = flipped[
                        p * N : p * N + N
                    ]
        snd[2 * layer + 1] = blk[...].reshape(N, 8, 128).astype(BF16)

    def spectral_rows(layer):
        wide = rcv[2 * layer + 1].astype(F32).reshape(N // 2, 2, 8, 128)
        even, odd = wide[:, 0], wide[:, 1]
        low = iota((N // 2, 8, 128), 1) < 4
        a = jnp.where(low, even, pltpu.roll(odd, 4, 1)).reshape(CX, 128)
        b = jnp.where(low, pltpu.roll(even, 4, 1), odd).reshape(CX, 128)
        spec[pl.ds(0, 128), :] = a.T.astype(BF16)
        spec[pl.ds(128, 128), :] = b.T.astype(BF16)

    def forward_send(layer):
        even, odd = pack_rows()
        view = snd.at[2 * layer]
        for i in range(N // 2):
            view[2 * i] = even[i]
            view[2 * i + 1] = odd[i]

    modes[...] = jnp.zeros_like(modes)
    for i in range(CHUNKS):
        cols = pl.ds(i * width, width)
        loads[i][0].wait()
        loads[i][1].wait()
        modes[...] += dot_nt(ft[:, cols], h[:, cols])

    load_taps.wait()
    load_bias.wait()
    conv_matrices(0)
    pl.semaphore_wait(barrier, N)

    def one_layer(layer, carry):
        forward_send(layer)
        exchange(2 * layer)
        edges_out(layer)
        shift_field()

        @pl.when(layer == 0)
        def _():
            load_rt.wait()
            load_wt.wait()
            load_bt.wait()
            conv_matrices(1)

        convolve(layer, range(1), edge=False)
        exchange_done(2 * layer)
        mix(layer)
        mixed_copy(layer).wait()
        back_rows(layer)
        exchange(2 * layer + 1)
        edges_in(layer)
        convolve(layer, range(1), main=False)
        convolve(layer, range(1, TILES))
        exchange_done(2 * layer + 1)
        spectral_rows(layer)

        @pl.when(layer < LAYERS - 1)
        def _():
            modes[...] = jnp.zeros_like(modes)
            for t, cols, product in column_pieces(spec, ft):
                h[:, cols] = gelu_of_half(acc[:, cols] + product).astype(BF16)
                if t % 4 == 3:
                    done = pl.ds((t - 3) * PIECE, 4 * PIECE)
                    modes[...] += dot_nt(ft[:, done], h[:, done])

        return carry

    lax.fori_loop(0, LAYERS, one_layer, 0)
    for index in range(2 * LAYERS):
        sent = snd.at[index, pl.ds(0, N - 1)]
        pltpu.make_async_copy(sent, sent, a_send.at[index]).wait()


def column_pieces(spec, ft):
    ahead = dot(spec[...], ft[:, pl.ds(0, PIECE)])
    for t in range(PIECES):
        now = ahead
        if t + 1 < PIECES:
            ahead = dot(spec[...], ft[:, pl.ds((t + 1) * PIECE, PIECE)])
        yield t, pl.ds(t * PIECE, PIECE), now


def finish(acc, ft, spec, out, h, o_sem):
    copies = []
    for t, cols, product in column_pieces(spec, ft):
        h[:, cols] = gelu_of_half(acc[:, cols] + product).astype(BF16)
        copies.append(pltpu.make_async_copy(h.at[:, cols], out.at[:, cols], o_sem.at[t]))
        copies[-1].start()
    for copy in copies:
        copy.wait()


def body(field, spec_weight, conv_weight, bias):
    flat = field.reshape(CX, NY)
    weight = spec_weight.reshape(LAYERS, 2, CG, 64, 128)
    taps = conv_weight.reshape(LAYERS, 3, 3, CG, CG)
    anywhere = pl.BlockSpec(memory_space=pl.ANY)
    rows = row_table()
    tables = [jnp.asarray(each) for each in (column_table(), rows, np.ascontiguousarray(rows.T))]
    operands = [flat, *tables, weight, taps, bias]
    operands = [pltpu.with_memory_space_constraint(each, pltpu.HBM) for each in operands]
    vmem = pl.BlockSpec(memory_space=pltpu.VMEM)
    acc, ft, spec = pl.pallas_call(
        kernel,
        out_shape=[
            pltpu.VMEM((CX, NY), F32),
            pltpu.VMEM((2 * M, NY), BF16),
            pltpu.VMEM((CX, 2 * M), BF16),
        ],
        in_specs=[anywhere] * 7,
        out_specs=[vmem] * 3,
        scratch_shapes=[
            pltpu.VMEM((CX, NY), BF16),
            pltpu.VMEM((XR * 2 * N, 2 * M), BF16),
            pltpu.VMEM((2 * M, XR * 2 * N), BF16),
            pltpu.VMEM((LAYERS, 2, CG, 64, 128), F32),
            pltpu.VMEM((LAYERS, 3, 3, CG, CG), BF16),
            pltpu.VMEM((LAYERS, CG), F32),
            pltpu.VMEM((LAYERS, CX, 1), F32),
            pltpu.VMEM((CX, NY), BF16),
            pltpu.VMEM((CX, NY), BF16),
            pltpu.VMEM((2 * M, CX), F32),
            pltpu.VMEM((2 * LAYERS, N, 8, 128), BF16),
            pltpu.VMEM((2 * LAYERS, N, 8, 128), BF16),
            pltpu.VMEM((N * 8, 128), F32),
            pltpu.VMEM((4, 128, 128), F32),
            pltpu.VMEM((32, XR * 128), BF16),
            pltpu.VMEM((32, 256), F32),
            pltpu.VMEM((LAYERS, 2, 32, 128), F32),
            pltpu.VMEM((LAYERS, 2, 32, 128), F32),
            pltpu.VMEM((2, 32, 128), F32),
            pltpu.VMEM((LAYERS, 3, CX, CX), BF16),
            pltpu.VMEM((LAYERS, CX, 128), BF16),
            pltpu.VMEM((LAYERS, 2, CG, NY), BF16),
            pltpu.VMEM((LAYERS, 2, CG, NY), BF16),
            pltpu.VMEM((128, NY), BF16),
            pltpu.SemaphoreType.DMA((2 * CHUNKS + 5,)),
            pltpu.SemaphoreType.DMA((2 * LAYERS,)),
            pltpu.SemaphoreType.DMA((2 * LAYERS,)),
            pltpu.SemaphoreType.DMA((LAYERS,)),
            pltpu.SemaphoreType.DMA((LAYERS,)),
            pltpu.SemaphoreType.DMA((LAYERS, 2)),
            pltpu.SemaphoreType.DMA((LAYERS, 2)),
        ],
        compiler_params=pltpu.CompilerParams(
            collective_id=0, has_side_effects=True, vmem_limit_bytes=40 * 2**20
        ),
        cost_estimate=pl.CostEstimate(
            flops=6 * 10**9, bytes_accessed=10 * 2**20, transcendentals=2 * CX * NY
        ),
        name="fourier_layers",
    )(*operands)
    result = pl.pallas_call(
        finish,
        out_shape=jax.ShapeDtypeStruct((CX, NY), BF16),
        in_specs=[vmem] * 3,
        out_specs=anywhere,
        scratch_shapes=[pltpu.VMEM((CX, NY), BF16), pltpu.SemaphoreType.DMA((PIECES,))],
        compiler_params=pltpu.CompilerParams(vmem_limit_bytes=16 * 2**20),
        name="last_rows",
    )(acc, ft, spec)
    return result.reshape(CG, XR, NY)


def solution(mesh):
    in_specs = (
        P("chan", "rows", None),
        P(None, None, "chan", None, "rows", None),
        P(None, "chan", None, None, None, None),
        P(None, "chan"),
    )
    out_specs = P("chan", "rows", None)
    return jax.shard_map(body, mesh=mesh, in_specs=in_specs, out_specs=out_specs, check_vma=False)
```
